256 devices in a mesh: scan: 8 (over x, y_hi), tile: 32 (over y_lo, z, core).
Axes of the slice: x: 4, y: 4 (y_hi: 2, y_lo: 2; y = y_hi * 2 + y_lo), z: 8, core: 2. Of those that a mesh axis runs over, the one named last changes fastest.
Arguments:
- object_field: float32 [2, 8192, 512], P(None, 'tile'), may hold values from -6 to 6
- probe: float32 [2, 256, 256], replicated, may hold values from -18 to 18
- amplitudes: bfloat16 [8, 32, 12, 256, 256], P('scan', 'tile'), may hold values from 0 to 6
- positions: int32 [8, 32, 12, 2], P('scan', 'tile'), may hold values from 0 to 7936, as said below
- counts: int32 [8, 32], P('scan', 'tile'), may hold values from 1 to 12, as said below
Outputs:
- new_object: float32 [2, 8192, 512], P(None, 'tile')
- new_probe: float32 [2, 256, 256], replicated
- probe_gradient: float32 [2, 256, 256], replicated
The draws below stay inside these ranges and needn't reach their ends.
Inputs may be any that keep to these rules, and one draw needn't show every extreme that they name: `positions`: every slot of the device at tile t names a window whose first row lies in rows t * 256 to (t + 1) * 256 - 1 and is at most 7936, and whose first column is at most 256; both ends are reached. `counts`: slots at and beyond a device's count are ignored; some device has exactly 12 live slots.
All inputs are finite; a program needn't handle non-finite values.
Results may differ from the reference program's by a relative error of at most 0.0065.
Values may be sent and summed in bfloat16 or wider, within the bound.
No kernel may reach another device: no remote copies, remote signals or barrier semaphores. Data moves between devices by JAX's collectives and lax.ppermute only.
A program may use at most 64 MiB of HBM per device.

```python
import math
import jax
import jax.numpy as jnp
from jax import lax

PS = 256
TH = 256
OW = 512
CAP = 12
ITERS = 2
NY = 8192
N_SCAN = 8
N_TILE = 32


def draw_probe(key, part):
    key = jax.random.fold_in(key, 7)
    first, second, third = jax.random.split(key, 3)
    row_scale = jnp.exp(jax.random.uniform(first, (PS,), jnp.float32, -0.8, 0.8))
    col_scale = jnp.exp(jax.random.uniform(second, (PS,), jnp.float32, -0.8, 0.8))
    base = jnp.clip(jax.random.normal(third, (2, PS, PS), jnp.float32), -3.5, 3.5)
    return base * row_scale[None, :, None] * col_scale[None, None, :]


def draw_positions(key, part):
    key = jax.random.fold_in(key, 5)
    first, second = jax.random.split(key)
    tiles = jnp.arange(N_TILE, dtype=jnp.int32)[None, :, None]
    reach = jnp.where(tiles == N_TILE - 1, TH - PS + 1, TH)
    offsets = jax.random.randint(first, (N_SCAN, N_TILE, CAP), 0, 1 << 20, dtype=jnp.int32) % reach
    rows_drawn = tiles * TH + offsets
    cols_drawn = jax.random.randint(second, (N_SCAN, N_TILE, CAP), 0, OW - PS + 1, dtype=jnp.int32)
    rows_drawn = rows_drawn.at[0, N_TILE - 1, 0].set(NY - PS)
    cols_drawn = cols_drawn.at[0, N_TILE - 1, 0].set(OW - PS)
    return jnp.stack([rows_drawn, cols_drawn], -1).astype(jnp.int32)


def draw_counts(key, part):
    key = jax.random.fold_in(key, 11)
    first, second, third, fourth = jax.random.split(key, 4)
    per_tile = jax.random.randint(first, (1, N_TILE), 0, CAP, dtype=jnp.int32)
    per_device = jax.random.randint(second, (N_SCAN, N_TILE), 0, CAP, dtype=jnp.int32)
    drawn = 1 + per_tile * per_device // max(CAP - 1, 1)
    pick_scan = jax.random.randint(third, (), 0, N_SCAN, dtype=jnp.int32)
    pick_tile = jax.random.randint(fourth, (), 0, N_TILE, dtype=jnp.int32)
    marked = (jnp.arange(N_SCAN, dtype=jnp.int32)[:, None] == pick_scan) & (jnp.arange(N_TILE, dtype=jnp.int32)[None, :] == pick_tile)
    return jnp.where(marked, CAP, drawn).astype(jnp.int32)


def block_levels(stream_key, extent, cuts, low, largest):
    def one(axis_at, blocks):
        steps = jax.random.uniform(jax.random.fold_in(jax.random.fold_in(stream_key, 6), axis_at), (blocks,), jnp.float32, low / len(cuts), largest / len(cuts))
        return jnp.repeat(jnp.exp(steps), extent[axis_at] // blocks).reshape((-1,) + (1,) * (len(extent) - axis_at - 1))

    loudness = one(*cuts[0])
    for cut in cuts[1:]:
        loudness = loudness * one(*cut)
    return loudness


def noise(stream_key, dims, spread, most, cuts=(), kind=jnp.bfloat16):
    array = jax.random.normal(stream_key, dims, jnp.float32) * spread
    if len(cuts) > 0:
        array = block_levels(stream_key, dims, cuts, -0.22, 0.18) * array
    return jnp.clip(array, min=-most, max=most).astype(kind)


def setup_inputs(seed: int = 0) -> dict:
    keys = jax.random.split(jax.random.key(seed), 6)
    return {
        "object_field": noise(keys[0], (2, NY, OW), 1.0, 6.0, ((1, 32),), jnp.float32),
        "probe": draw_probe(jax.random.fold_in(keys[5], 71), 0),
        "amplitudes": jnp.clip(6.0 * jax.random.uniform(keys[2], (N_SCAN, N_TILE, CAP, PS, PS), jnp.float32) ** block_levels(keys[2], (N_SCAN, N_TILE, CAP, PS, PS), ((0, 8), (1, 32)), -0.2, 0.2), 0.0, 6.0).astype(jnp.bfloat16),
        "positions": draw_positions(jax.random.fold_in(keys[5], 71), 0),
        "counts": draw_counts(jax.random.fold_in(keys[5], 71), 0),
    }


floor_level = 0.5
regular = 1.0

def dft_tables(length):
    indices = jnp.arange(length, dtype=jnp.int32)
    phases = indices[:, None] * indices[None, :] % length
    angles = phases.astype(jnp.float32) * (2.0 * math.pi / length)
    factor = 1.0 / math.sqrt(length)
    return ((jnp.cos(angles) * factor).astype(jnp.bfloat16), (jnp.sin(angles) * factor).astype(jnp.bfloat16))

def right_apply(real_part, imag_part, cosine_table, sine_table, orient):
    rows_count = real_part.shape[0]
    stacked = jnp.concatenate([real_part, imag_part], 0)
    with_cos = jnp.dot(stacked, cosine_table, preferred_element_type=jnp.float32)
    with_sin = jnp.dot(stacked, sine_table, preferred_element_type=jnp.float32)
    out_real = with_cos[:rows_count] - orient * with_sin[rows_count:]
    out_imag = with_cos[rows_count:] + orient * with_sin[:rows_count]
    return (out_real, out_imag)

def left_apply(real_part, imag_part, cosine_table, sine_table, orient):
    cols_count = real_part.shape[1]
    stacked = jnp.concatenate([real_part, imag_part], 1)
    with_cos = jnp.dot(cosine_table, stacked, preferred_element_type=jnp.float32)
    with_sin = jnp.dot(sine_table, stacked, preferred_element_type=jnp.float32)
    out_real = with_cos[:, :cols_count] - orient * with_sin[:, cols_count:]
    out_imag = with_cos[:, cols_count:] + orient * with_sin[:, :cols_count]
    return (out_real, out_imag)

def transform(real_part, imag_part, cosine_table, sine_table, orient):
    half_real, half_imag = right_apply(real_part, imag_part, cosine_table, sine_table, orient)
    return left_apply(half_real.astype(jnp.bfloat16), half_imag.astype(jnp.bfloat16), cosine_table, sine_table, orient)

def pattern_terms(patch_real, patch_imag, probe_real, probe_imag, measured, cosine_table, sine_table):
    wave_real = probe_real * patch_real - probe_imag * patch_imag
    wave_imag = probe_real * patch_imag + probe_imag * patch_real
    far_real, far_imag = transform(wave_real.astype(jnp.bfloat16), wave_imag.astype(jnp.bfloat16), cosine_table, sine_table, -1.0)
    magnitude = jnp.sqrt(far_real * far_real + far_imag * far_imag)
    rescale = measured.astype(jnp.float32) / jnp.maximum(magnitude, floor_level) - 1.0
    back_real, back_imag = transform((rescale * far_real).astype(jnp.bfloat16), (rescale * far_imag).astype(jnp.bfloat16), cosine_table, sine_table, 1.0)
    object_real = probe_real * back_real + probe_imag * back_imag
    object_imag = probe_real * back_imag - probe_imag * back_real
    probe_real_term = patch_real * back_real + patch_imag * back_imag
    probe_imag_term = patch_real * back_imag - patch_imag * back_real
    intensity = patch_real * patch_real + patch_imag * patch_imag
    return (object_real, object_imag, probe_real_term, probe_imag_term, intensity)

def reference(object_field, probe, amplitudes, positions, counts):
    cosine_table, sine_table = dft_tables(PS)
    corners = positions.reshape(-1, 2)
    measured_all = amplitudes.reshape(-1, PS, PS)
    active_all = (jnp.arange(CAP, dtype=jnp.int32)[None, None, :] < counts[:, :, None]).reshape(-1)
    anchor = jnp.zeros((), jnp.int32)
    current_object = object_field
    current_probe = probe
    last_gradient = jnp.zeros((2, PS, PS), jnp.float32)
    for sweep in range(ITERS):
        illumination_map = current_probe[0] * current_probe[0] + current_probe[1] * current_probe[1]

        def visit(partial_value, element, current_object=current_object, current_probe=current_probe, illumination_map=illumination_map):
            corner, measured, active = element

            def accumulate(carried):
                gradients, probe_sums = carried
                window = lax.dynamic_slice(current_object, (anchor, corner[0], corner[1]), (2, PS, PS))
                terms = pattern_terms(window[0], window[1], current_probe[0], current_probe[1], measured, cosine_table, sine_table)
                previous = lax.dynamic_slice(gradients, (anchor, corner[0], corner[1]), (3, PS, PS))
                added = previous + jnp.stack([terms[0], terms[1], illumination_map])
                gradients = lax.dynamic_update_slice(gradients, added, (anchor, corner[0], corner[1]))
                return (gradients, probe_sums + jnp.stack([terms[2], terms[3], terms[4]]))
            return (lax.cond(active, accumulate, lambda carried: carried, partial_value), None)
        start = (jnp.zeros((3, NY, OW), jnp.float32), jnp.zeros((3, PS, PS), jnp.float32))
        (gradients, probe_sums), _ = lax.scan(visit, start, (corners, measured_all, active_all))
        current_object = current_object + gradients[:2] / (gradients[2] + regular)
        current_probe = current_probe + probe_sums[:2] / (probe_sums[2] + regular)
        last_gradient = probe_sums[:2] / jnp.sqrt(probe_sums[2] + regular)
    return (current_object, current_probe, last_gradient)
```

```python
import functools
import math

import jax
import jax.numpy as jnp
import numpy as np
from jax import lax
from jax.experimental import pallas as pl
from jax.experimental.pallas import tpu as pltpu
from jax.sharding import PartitionSpec as P

ITERS = 2
PS = 256
TH = 256
OW = 512
CAP = 12
NS = 8
NT = 32
SR = TH // NS
CH = 64
LN = 128
FLOOR2 = 0.25
REG = 1.0

OWN, NEXT, PRB, POS = 0, 2 * SR, 4 * SR, 4 * SR + 48
SEND = POS + 16
GROUP = 12

BF = jnp.bfloat16
F32 = jnp.float32
VMEM_LIMIT = 56 * 1024 * 1024


def tables():
    n = np.arange(PS, dtype=np.int64)
    angle = ((n[:, None] * n[None, :]) % PS).astype(np.float32) * np.float32(2.0 * math.pi / PS)
    c = (np.cos(angle) / np.sqrt(PS)).astype(np.float32)
    s = (np.sin(angle) / np.sqrt(PS)).astype(np.float32)
    return c, s


def table_arrays():
    c, s = tables()
    m1 = np.block([[c, -s], [s, c]])
    m2 = np.block([[c, s], [-s, c]])

    def grouped(m):
        rows = m.reshape(2, PS // CH, CH, 2 * PS)
        return rows.transpose(1, 0, 2, 3).reshape(2 * PS, 2 * PS)

    return [jnp.asarray(t.astype(jnp.bfloat16)) for t in (m1, m2, grouped(m2), grouped(m1))]


def pattern_kernel(
    first, pos_ref, cnt_ref, obj_ref, halo_ref, probe_ref, amp_ref, posblk_ref, m1_ref, m2_ref, a1_ref, a2_ref, *rest
):
    if first:
        send_ref, x, pr, g, pg, patch, h, h2 = rest
    else:
        recv_ref, send_ref, objn_ref, probn_ref, x, pr, g, pg, patch, h, h2 = rest
    tile_start = lax.axis_index("tile") * TH
    if first:
        for q in range(4):
            x[:, q, :TH, :] = obj_ref[:, :, q * LN : (q + 1) * LN]
            x[:, q, TH:, :] = halo_ref[:, :, q * LN : (q + 1) * LN].astype(F32)
        pr[...] = probe_ref[...]
    else:
        for s in range(NS):
            for k in range(2):
                a = s * SR
                new = obj_ref[k, a : a + SR, :] + recv_ref[s, k * SR : (k + 1) * SR, :].astype(F32)
                objn_ref[k, a : a + SR, :] = new
                low = halo_ref[k, a : a + SR, :].astype(F32) + recv_ref[s, (2 + k) * SR : (3 + k) * SR, :].astype(F32)
                for q in range(4):
                    x[k, q, a : a + SR, :] = new[:, q * LN : (q + 1) * LN]
                    x[k, q, TH + a : TH + a + SR, :] = low[:, q * LN : (q + 1) * LN]
                d = recv_ref[s, 4 * SR + 16 * k : 4 * SR + 16 * (k + 1), :].astype(F32)
                for q in range(2):
                    b = a + 16 * q
                    new = probe_ref[k, b : b + 16, :] + d[:, q * PS : (q + 1) * PS]
                    pr[k, b : b + 16, :] = new
                    probn_ref[k, b : b + 16, :] = new
    g[...] = jnp.zeros_like(g)
    pg[...] = jnp.zeros_like(pg)

    def visit(j, carry):
        r = pos_ref[j, 0] - tile_start
        c = pos_ref[j, 1]
        base = jnp.where(c >= LN, 1, 0)
        off = c - base * LN
        lanes = lax.broadcasted_iota(jnp.int32, (CH, LN), 1)
        head = lanes < LN - off
        tail = lanes >= off
        to_left = (LN - off) & (LN - 1)
        to_right = off & (LN - 1)
        for i in range(PS // CH):
            a = i * CH
            xs = []
            for k in range(2):
                v = [pltpu.roll(x[k, base + q, pl.ds(r + a, CH), :], to_left, 1) for q in range(3)]
                v = jnp.concatenate([jnp.where(head, v[0], v[1]), jnp.where(head, v[1], v[2])], 1)
                patch[k, a : a + CH, :] = v
                xs.append(v)
            xr, xi = xs
            p0 = pr[0, a : a + CH, :]
            p1 = pr[1, a : a + CH, :]
            pg[2, a : a + CH, :] += xr * xr + xi * xi
            w = jnp.concatenate([(p0 * xr - p1 * xi).astype(BF), (p0 * xi + p1 * xr).astype(BF)], 1)
            half = jnp.dot(w, m1_ref[...], preferred_element_type=F32).astype(BF)
            h[a : a + CH, :] = half[:, :PS]
            h[PS + a : PS + a + CH, :] = half[:, PS:]
        for i in range(PS // CH):
            a = i * CH
            far = jnp.dot(a1_ref[2 * a : 2 * a + 2 * CH, :], h[...], preferred_element_type=F32)
            fr = far[:CH]
            fi = far[CH:]
            m = jnp.maximum(fr * fr + fi * fi, FLOOR2)
            q = amp_ref[j, a : a + CH, :].astype(F32) * lax.rsqrt(m) - 1.0
            u = jnp.concatenate([(q * fr).astype(BF), (q * fi).astype(BF)], 1)
            half = jnp.dot(u, m2_ref[...], preferred_element_type=F32).astype(BF)
            h2[a : a + CH, :] = half[:, :PS]
            h2[PS + a : PS + a + CH, :] = half[:, PS:]
        for i in range(PS // CH):
            a = i * CH
            back = jnp.dot(a2_ref[2 * a : 2 * a + 2 * CH, :], h2[...], preferred_element_type=F32)
            br = back[:CH]
            bi = back[CH:]
            xr = patch[0, a : a + CH, :]
            xi = patch[1, a : a + CH, :]
            pg[0, a : a + CH, :] += xr * br + xi * bi
            pg[1, a : a + CH, :] += xr * bi - xi * br
            p0 = pr[0, a : a + CH, :]
            p1 = pr[1, a : a + CH, :]
            for k, o in enumerate((p0 * br + p1 * bi, p0 * bi - p1 * br)):
                v = [pltpu.roll(o[:, q * LN : (q + 1) * LN], to_right, 1) for q in range(2)]
                g[k, base, pl.ds(r + a, CH), :] += jnp.where(tail, v[0], 0.0)
                g[k, base + 1, pl.ds(r + a, CH), :] += jnp.where(tail, v[1], v[0])
                g[k, base + 2, pl.ds(r + a, CH), :] += jnp.where(tail, 0.0, v[1])
        return carry

    lax.fori_loop(0, cnt_ref[0], visit, 0)
    for s in range(NS):
        a = s * SR
        for k in range(2):
            for q in range(4):
                cols = slice(q * LN, (q + 1) * LN)
                send_ref[s, OWN + k * SR : OWN + (k + 1) * SR, cols] = g[k, q, a : a + SR, :].astype(BF)
                send_ref[s, NEXT + k * SR : NEXT + (k + 1) * SR, cols] = g[k, q, TH + a : TH + a + SR, :].astype(BF)
        for k in range(3):
            send_ref[s, PRB + 16 * k : PRB + 16 * (k + 1), :] = jnp.concatenate(
                [pg[k, a : a + 16, :], pg[k, a + 16 : a + 32, :]], 1
            ).astype(BF)
        send_ref[s, POS:, :] = posblk_ref[...]


def smem():
    return pl.BlockSpec(memory_space=pltpu.SMEM)


def vmem():
    return pl.BlockSpec(memory_space=pltpu.VMEM)


def params():
    return pltpu.CompilerParams(vmem_limit_bytes=VMEM_LIMIT)


def patterns(pos, cnt, obj, halo, probe, amps, posblk, tabs, recv=None):
    first = recv is None
    out = [jax.ShapeDtypeStruct((NS, SEND, OW), BF)]
    if not first:
        out += [jax.ShapeDtypeStruct((2, TH, OW), F32), jax.ShapeDtypeStruct((2, PS, PS), F32)]
    args = [pos, cnt, obj, halo, probe, amps, posblk, *tabs] + ([] if first else [recv])
    return pl.pallas_call(
        functools.partial(pattern_kernel, first),
        out_shape=out,
        in_specs=[smem(), smem()] + [vmem()] * (len(args) - 2),
        out_specs=[vmem()] * len(out),
        scratch_shapes=[
            pltpu.VMEM((2, 4, 2 * TH, LN), F32),
            pltpu.VMEM((2, PS, PS), F32),
            pltpu.VMEM((2, 4, 2 * TH, LN), F32),
            pltpu.VMEM((3, PS, PS), F32),
            pltpu.VMEM((2, PS, PS), F32),
            pltpu.VMEM((2 * PS, PS), BF),
            pltpu.VMEM((2 * PS, PS), BF),
        ],
        compiler_params=params(),
        name="patterns",
    )(*args)


def sum_kernel(recv_ref, own_ref, next_ref, probe_ref, up_ref, down_ref, pos_ref):
    def total(a, n):
        t = recv_ref[0, a : a + n, :].astype(F32)
        for s in range(1, NS):
            t = t + recv_ref[s, a : a + n, :].astype(F32)
        return t

    own = total(OWN, 2 * SR)
    own_ref[...] = own
    down_ref[: 2 * SR, :] = own.astype(BF)
    nxt = total(NEXT, 2 * SR)
    next_ref[...] = nxt
    up_ref[: 2 * SR, :] = nxt.astype(BF)
    probe_ref[...] = total(PRB, 48)
    pos = total(POS, 16)
    pos_ref[...] = pos[:, :128]
    up_ref[2 * SR :, :] = pos.astype(BF)
    down_ref[2 * SR :, :] = pos.astype(BF)


def sums(recv):
    return pl.pallas_call(
        sum_kernel,
        out_shape=[
            jax.ShapeDtypeStruct((2 * SR, OW), F32),
            jax.ShapeDtypeStruct((2 * SR, OW), F32),
            jax.ShapeDtypeStruct((48, OW), F32),
            jax.ShapeDtypeStruct((2 * SR + 16, OW), BF),
            jax.ShapeDtypeStruct((2 * SR + 16, OW), BF),
            jax.ShapeDtypeStruct((16, 128), F32),
        ],
        in_specs=[vmem()],
        out_specs=[vmem()] * 6,
        compiler_params=params(),
        name="sums",
    )(recv)


def illum_kernel(last, pos_ref, probe_ref, out_ref, p2, acc):
    for q in range(2):
        cols = slice(q * LN, (q + 1) * LN)
        p2[q, :SR, :] = jnp.zeros((SR, LN), F32)
        p2[q, SR + PS :, :] = jnp.zeros((SR, LN), F32)
        p2[q, SR : SR + PS, :] = probe_ref[0, :, cols] * probe_ref[0, :, cols] + probe_ref[1, :, cols] * probe_ref[1, :, cols]
    acc[...] = jnp.zeros_like(acc)
    mine = lax.axis_index("scan") * SR

    for shift in (-1, 0) if last else (-1, 0, 1):

        def group(s, carry, shift=shift):
            row = (shift + 1) * NS + s

            def one(j, carry):
                first = pos_ref[row, j] + (shift * TH - 1)
                c = pos_ref[row, GROUP + j]
                base = jnp.where(c >= LN, 1, 0)
                off = c - base * LN
                tail = lax.broadcasted_iota(jnp.int32, (SR, LN), 1) >= off
                to_right = off & (LN - 1)
                for block in (0,) if last or shift < 0 else (0, 1) if shift == 0 else (1,):
                    at = mine + block * TH - first

                    @pl.when((at > -SR) & (at < PS))
                    def _(at=at, block=block):
                        v = [pltpu.roll(p2[q, pl.ds(at + SR, SR), :], to_right, 1) for q in range(2)]
                        acc[block, base] += jnp.where(tail, v[0], 0.0)
                        acc[block, base + 1] += jnp.where(tail, v[1], v[0])
                        acc[block, base + 2] += jnp.where(tail, 0.0, v[1])

                return carry

            lax.fori_loop(0, pos_ref[row, 2 * GROUP], one, 0)
            return carry

        lax.fori_loop(0, NS, group, 0)
    for block in range(1 if last else 2):
        for q in range(4):
            out_ref[block, :, q * LN : (q + 1) * LN] = acc[block, q]


def illumination(last, pos, probe):
    blocks = 1 if last else 2
    return pl.pallas_call(
        functools.partial(illum_kernel, last),
        out_shape=jax.ShapeDtypeStruct((blocks, SR, OW), F32),
        in_specs=[smem(), vmem()],
        out_specs=vmem(),
        scratch_shapes=[pltpu.VMEM((2, PS + 2 * SR, LN), F32), pltpu.VMEM((blocks, 4, SR, LN), F32)],
        compiler_params=params(),
        name="illumination",
    )(pos, probe)


def step_kernel(last, *refs):
    if last:
        own_ref, up_ref, ill_ref, probe_ref, out_ref = refs
    else:
        own_ref, up_ref, ill_ref, probe_ref, next_ref, down_ref, out_ref = refs
    scale = 1.0 / (ill_ref[0] + REG)
    w = probe_ref[32:48, :] + REG
    parts = []
    for k in range(2):
        a = k * SR
        parts.append((own_ref[a : a + SR, :] + up_ref[a : a + SR, :].astype(F32)) * scale)
    if last:
        root = jnp.sqrt(w)
        parts += [probe_ref[:16, :] / root, probe_ref[16:32, :] / root, root]
    else:
        scale = 1.0 / (ill_ref[1] + REG)
        for k in range(2):
            a = k * SR
            parts.append((next_ref[a : a + SR, :] + down_ref[a : a + SR, :].astype(F32)) * scale)
        parts += [probe_ref[:16, :] / w, probe_ref[16:32, :] / w]
    at = 0
    for part in parts:
        n = part.shape[0]
        part = part.astype(BF)
        for s in range(NS):
            out_ref[s, at : at + n, :] = part
        at += n


def steps(last, own, up, ill, probe, nxt, down):
    rows = 2 * SR + 48 if last else 4 * SR + 32
    args = [own, up, ill, probe] + ([] if last else [nxt, down])
    return pl.pallas_call(
        functools.partial(step_kernel, last),
        out_shape=jax.ShapeDtypeStruct((NS, rows, OW), BF),
        in_specs=[vmem()] * len(args),
        out_specs=vmem(),
        compiler_params=params(),
        name="steps",
    )(*args)


def final_kernel(obj_ref, probe_ref, recv_ref, obj_out, probe_out, grad_out):
    for s in range(NS):
        a = s * SR
        root = recv_ref[s, 2 * SR + 32 : 2 * SR + 48, :].astype(F32)
        for k in range(2):
            obj_out[k, a : a + SR, :] = obj_ref[k, a : a + SR, :] + recv_ref[s, k * SR : (k + 1) * SR, :].astype(F32)
            grad = recv_ref[s, 2 * SR + 16 * k : 2 * SR + 16 * (k + 1), :].astype(F32)
            d = grad / root
            for q in range(2):
                b = a + 16 * q
                grad_out[k, b : b + 16, :] = grad[:, q * PS : (q + 1) * PS]
                probe_out[k, b : b + 16, :] = probe_ref[k, b : b + 16, :] + d[:, q * PS : (q + 1) * PS]


def final(obj, probe, recv):
    return pl.pallas_call(
        final_kernel,
        out_shape=[
            jax.ShapeDtypeStruct((2, TH, OW), F32),
            jax.ShapeDtypeStruct((2, PS, PS), F32),
            jax.ShapeDtypeStruct((2, PS, PS), F32),
        ],
        in_specs=[vmem()] * 3,
        out_specs=[vmem()] * 3,
        compiler_params=params(),
        name="final",
    )(obj, probe, recv)


def shifted(block, distance):
    return lax.ppermute(block, "tile", [(i, i + distance) for i in range(NT) if 0 <= i + distance < NT])


def tile_sum(x):
    for d in (1, 2, 4, 8, 16):
        x = x + lax.ppermute(x, "tile", [(i, i ^ d) for i in range(NT)])
    return x


def exchange(blocks):
    return lax.all_to_all(blocks, "scan", 0, 0, tiled=True)


def on_device(object_field, probe, amplitudes, positions, counts):
    tabs = table_arrays()
    pos = positions[0, 0]
    cnt = counts[0, 0].reshape(1)
    amps = amplitudes[0, 0]
    halo = shifted(object_field.astype(BF), -1)
    row = jnp.concatenate([pos[:, 0] - lax.axis_index("tile") * TH + 1, pos[:, 1], cnt])
    mine = lax.broadcasted_iota(jnp.int32, (16, 1), 0) == lax.axis_index("scan")
    posblk = jnp.where(mine, row[None, :], 0).astype(BF)
    posblk = jnp.pad(posblk, ((0, 0), (0, OW - row.shape[0])))
    recv = None
    for sweep in range(ITERS):
        last = sweep == ITERS - 1
        if sweep == 0:
            (send,) = patterns(pos, cnt, object_field, halo, probe, amps, posblk, tabs)
        else:
            send, object_field, probe = patterns(pos, cnt, object_field, halo, probe, amps, posblk, tabs, recv)
        own, nxt, psum, up, down, tile_pos = sums(exchange(send))
        up = shifted(up, 1)
        if sweep == 0:
            down = shifted(down, -1)
            around = jnp.concatenate(
                [up[2 * SR :, : 2 * GROUP + 1][:NS].astype(F32), tile_pos[:NS, : 2 * GROUP + 1], down[2 * SR :, : 2 * GROUP + 1][:NS].astype(F32)], 0
            ).astype(jnp.int32)
        ill = illumination(last, around, probe)
        total = tile_sum(psum)
        recv = exchange(steps(last, own, up, ill, total, nxt, down))
    return tuple(final(object_field, probe, recv))


def solution(mesh):
    in_specs = (
        P(None, "tile", None),
        P(),
        P("scan", "tile", None, None, None),
        P("scan", "tile", None, None),
        P("scan", "tile"),
    )
    out_specs = (P(None, "tile", None), P(), P())
    return jax.shard_map(on_device, mesh=mesh, in_specs=in_specs, out_specs=out_specs, check_vma=False)
```

```python
import functools
import math

import jax
import jax.numpy as jnp
import numpy as np
from jax import lax
from jax.experimental import pallas as pl
from jax.experimental.pallas import tpu as pltpu
from jax.sharding import PartitionSpec as P

ITERS = 2
PS = 256
TH = 256
OW = 512
CAP = 12
NS = 8
NT = 32
SR = TH // NS
LN = 128
PAIR = 3
FLOOR2 = 0.25
REG = 1.0

OWN, NEXT, PRB, POS = 0, 2 * SR, 4 * SR, 4 * SR + 48
SEND = POS + 16
GROUP = 12

BF = jnp.bfloat16
F32 = jnp.float32
VMEM_LIMIT = 56 * 1024 * 1024


def tables():
    n = np.arange(PS, dtype=np.int64)
    angle = ((n[:, None] * n[None, :]) % PS).astype(np.float32) * np.float32(2.0 * math.pi / PS)
    c = (np.cos(angle) / np.sqrt(PS)).astype(np.float32)
    s = (np.sin(angle) / np.sqrt(PS)).astype(np.float32)
    return c, s


def table_arrays():
    c, s = tables()
    return [jnp.asarray(np.block(m).astype(jnp.bfloat16)) for m in ([[c, -s], [s, c]], [[c, s], [-s, c]])]


def pattern_kernel(first, pos_ref, cnt_ref, obj_ref, halo_ref, probe_ref, amp_ref, posblk_ref, m1_ref, m2_ref, *rest):
    if first:
        send_ref, x, pr, g, pg, patch, h, h2, amp, amp_sem = rest
    else:
        recv_ref, send_ref, objn_ref, probn_ref, x, pr, g, pg, patch, h, h2, amp, amp_sem = rest
    count = cnt_ref[0]
    copies = [pltpu.make_async_copy(amp_ref.at[j], amp.at[j], amp_sem.at[j]) for j in range(CAP)]
    for copy in copies:
        copy.start()
    tile_start = lax.axis_index("tile") * TH
    if first:
        for q in range(4):
            x[:, q, :TH, :] = obj_ref[:, :, q * LN : (q + 1) * LN]
            x[:, q, TH:, :] = halo_ref[:, :, q * LN : (q + 1) * LN].astype(F32)
        pr[...] = probe_ref[...]
    else:
        for s in range(NS):
            for k in range(2):
                a = s * SR
                new = obj_ref[k, a : a + SR, :] + recv_ref[s, k * SR : (k + 1) * SR, :].astype(F32)
                objn_ref[k, a : a + SR, :] = new
                low = halo_ref[k, a : a + SR, :].astype(F32) + recv_ref[s, (2 + k) * SR : (3 + k) * SR, :].astype(F32)
                for q in range(4):
                    x[k, q, a : a + SR, :] = new[:, q * LN : (q + 1) * LN]
                    x[k, q, TH + a : TH + a + SR, :] = low[:, q * LN : (q + 1) * LN]
                d = recv_ref[s, 4 * SR + 16 * k : 4 * SR + 16 * (k + 1), :].astype(F32)
                for q in range(2):
                    b = a + 16 * q
                    new = probe_ref[k, b : b + 16, :] + d[:, q * PS : (q + 1) * PS]
                    pr[k, b : b + 16, :] = new
                    probn_ref[k, b : b + 16, :] = new
    g[...] = jnp.zeros_like(g)
    pg[...] = jnp.zeros_like(pg)

    def place(j):
        r = pos_ref[0, j] - tile_start
        c = pos_ref[1, j]
        base = jnp.where(c >= LN, 1, 0)
        return r, base, c - base * LN

    lanes = lax.broadcasted_iota(jnp.int32, (PS, LN), 1)

    def to_half(j, slot, live):
        r, base, off = place(j)
        head = lanes < LN - off
        turn = (LN - off) & (LN - 1)
        xs = []
        for k in range(2):
            v = [pltpu.roll(x[k, base + q, pl.ds(r, PS), :], turn, 1) for q in range(3)]
            v = jnp.concatenate([jnp.where(head, v[0], v[1]), jnp.where(head, v[1], v[2])], 1)
            patch[slot, k] = v
            xs.append(v)
        xr, xi = xs
        p0, p1 = pr[0], pr[1]
        pg[2] += (xr * xr + xi * xi) * live
        w = jnp.concatenate([(p0 * xr - p1 * xi).astype(BF), (p0 * xi + p1 * xr).astype(BF)], 1)
        half = jnp.dot(w, m1_ref[...], preferred_element_type=F32).astype(BF)
        h[slot, :PS, :] = half[:, :PS]
        h[slot, PS:, :] = half[:, PS:]

    def to_back_half(j, slot, live):
        far = jnp.dot(m2_ref[...], h[slot], preferred_element_type=F32)
        fr, fi = far[:PS], far[PS:]
        m = jnp.maximum(fr * fr + fi * fi, FLOOR2)
        q = amp[j].astype(F32) * lax.rsqrt(m) - 1.0
        q = q * live
        u = jnp.concatenate([(q * fr).astype(BF), (q * fi).astype(BF)], 1)
        half = jnp.dot(u, m2_ref[...], preferred_element_type=F32).astype(BF)
        h2[slot, :PS, :] = half[:, :PS]
        h2[slot, PS:, :] = half[:, PS:]

    def add_back(j, slot):
        back = jnp.dot(m1_ref[...], h2[slot], preferred_element_type=F32)
        br, bi = back[:PS], back[PS:]
        xr, xi = patch[slot, 0], patch[slot, 1]
        pg[0] += xr * br + xi * bi
        pg[1] += xr * bi - xi * br
        p0, p1 = pr[0], pr[1]
        r, base, off = place(j)
        tail = lanes >= off
        turn = off & (LN - 1)
        for k, o in enumerate((p0 * br + p1 * bi, p0 * bi - p1 * br)):
            v = [pltpu.roll(o[:, q * LN : (q + 1) * LN], turn, 1) for q in range(2)]
            g[k, base, pl.ds(r, PS), :] += jnp.where(tail, v[0], 0.0)
            g[k, base + 1, pl.ds(r, PS), :] += jnp.where(tail, v[1], v[0])
            g[k, base + 2, pl.ds(r, PS), :] += jnp.where(tail, 0.0, v[1])

    for copy in copies:
        copy.wait()

    def visit(i, carry):
        j = [PAIR * i] + [jnp.minimum(PAIR * i + n, CAP - 1) for n in range(1, PAIR)]
        live = [jnp.where(PAIR * i + n < count, 1.0, 0.0) for n in range(PAIR)]
        for n in range(PAIR):
            to_half(j[n], n, live[n])
        for n in range(PAIR):
            to_back_half(j[n], n, live[n])
        for n in range(PAIR):
            add_back(j[n], n)
        return carry

    lax.fori_loop(0, (count + PAIR - 1) // PAIR, visit, 0)
    for s in range(NS):
        a = s * SR
        for k in range(2):
            for q in range(4):
                cols = slice(q * LN, (q + 1) * LN)
                send_ref[s, OWN + k * SR : OWN + (k + 1) * SR, cols] = g[k, q, a : a + SR, :].astype(BF)
                send_ref[s, NEXT + k * SR : NEXT + (k + 1) * SR, cols] = g[k, q, TH + a : TH + a + SR, :].astype(BF)
        for k in range(3):
            send_ref[s, PRB + 16 * k : PRB + 16 * (k + 1), :] = jnp.concatenate(
                [pg[k, a : a + 16, :], pg[k, a + 16 : a + 32, :]], 1
            ).astype(BF)
        send_ref[s, POS:, :] = posblk_ref[...]


def smem():
    return pl.BlockSpec(memory_space=pltpu.SMEM)


def vmem():
    return pl.BlockSpec(memory_space=pltpu.VMEM)


def params():
    return pltpu.CompilerParams(vmem_limit_bytes=VMEM_LIMIT)


def patterns(pos, cnt, obj, halo, probe, amps, posblk, tabs, recv=None):
    first = recv is None
    out = [jax.ShapeDtypeStruct((NS, SEND, OW), BF)]
    if not first:
        out += [jax.ShapeDtypeStruct((2, TH, OW), F32), jax.ShapeDtypeStruct((2, PS, PS), F32)]
    args = [pos, cnt, obj, halo, probe, amps, posblk, *tabs] + ([] if first else [recv])
    return pl.pallas_call(
        functools.partial(pattern_kernel, first),
        out_shape=out,
        in_specs=[smem(), smem()] + [vmem()] * 3 + [pl.BlockSpec(memory_space=pl.ANY)] + [vmem()] * (len(args) - 6),
        out_specs=[vmem()] * len(out),
        scratch_shapes=[
            pltpu.VMEM((2, 4, 2 * TH, LN), F32),
            pltpu.VMEM((2, PS, PS), F32),
            pltpu.VMEM((2, 4, 2 * TH, LN), F32),
            pltpu.VMEM((3, PS, PS), F32),
            pltpu.VMEM((PAIR, 2, PS, PS), F32),
            pltpu.VMEM((PAIR, 2 * PS, PS), BF),
            pltpu.VMEM((PAIR, 2 * PS, PS), BF),
            pltpu.VMEM((CAP, PS, PS), BF),
            pltpu.SemaphoreType.DMA((CAP,)),
        ],
        compiler_params=params(),
        name="patterns",
    )(*args)


def odd_tile():
    return lax.rem(lax.axis_index("tile"), 2) == 1


def sum_kernel(last, recv_ref, own_ref, next_ref, probe_ref, *rest):
    def total(a, n):
        t = recv_ref[0, a : a + n, :].astype(F32)
        for s in range(1, NS):
            t = t + recv_ref[s, a : a + n, :].astype(F32)
        return t

    own = total(OWN, 2 * SR)
    own_ref[...] = own
    nxt = total(NEXT, 2 * SR)
    next_ref[...] = nxt
    probe_ref[...] = total(PRB, 48).astype(BF)
    if last:
        (up_ref,) = rest
        up_ref[...] = nxt.astype(BF)
    else:
        inner_ref, outer_ref, pos_ref = rest
        odd = odd_tile()
        pos = total(POS, 16)
        pos_ref[...] = pos[:, :LN]
        inner_ref[: 2 * SR, :] = jnp.where(odd, own, nxt).astype(BF)
        outer_ref[: 2 * SR, :] = jnp.where(odd, nxt, own).astype(BF)
        inner_ref[2 * SR :, :] = pos.astype(BF)
        outer_ref[2 * SR :, :] = pos.astype(BF)


def sums(last, recv):
    out = [
        jax.ShapeDtypeStruct((2 * SR, OW), F32),
        jax.ShapeDtypeStruct((2 * SR, OW), F32),
        jax.ShapeDtypeStruct((48, OW), BF),
    ]
    if last:
        out += [jax.ShapeDtypeStruct((2 * SR, OW), BF)]
    else:
        out += [jax.ShapeDtypeStruct((2 * SR + 16, OW), BF)] * 2 + [jax.ShapeDtypeStruct((16, LN), F32)]
    return pl.pallas_call(
        functools.partial(sum_kernel, last),
        out_shape=out,
        in_specs=[vmem()],
        out_specs=[vmem()] * len(out),
        compiler_params=params(),
        name="sums",
    )(recv)


def illum_kernel(last, pos_ref, probe_ref, out_ref, p2):
    for q in range(2):
        cols = slice(q * LN, (q + 1) * LN)
        p2[q, :SR, :] = jnp.zeros((SR, LN), F32)
        p2[q, SR + PS :, :] = jnp.zeros((SR, LN), F32)
        p2[q, SR : SR + PS, :] = probe_ref[0, :, cols] * probe_ref[0, :, cols] + probe_ref[1, :, cols] * probe_ref[1, :, cols]
    mine = lax.axis_index("scan") * SR
    lanes = lax.broadcasted_iota(jnp.int32, (SR, LN), 1)
    zero = jnp.zeros((SR, LN), F32)

    def add(shift, blocks, carry):
        def group(s, carry):
            row = (shift + 1) * NS + s

            def some(i, carry):
                carry = [list(c) for c in carry]
                for n in range(4):
                    j = 4 * i + n
                    code = pos_ref[row, j]
                    first = jnp.where(code > 0, code + (shift * TH - 1), -4 * TH)
                    c = pos_ref[row, GROUP + j]
                    turn = c & (LN - 1)
                    masks = [lanes >= c - q * LN for q in range(4)]
                    ends = [lanes >= c + (2 - q) * LN for q in range(4)]
                    left = [lanes >= c + (1 - q) * LN for q in range(4)]
                    for b in blocks:
                        at = jnp.clip(mine + b * TH - first, -SR, PS) + SR
                        y0, y1 = (pltpu.roll(p2[q, pl.ds(at, SR), :], turn, 1) for q in range(2))
                        for q in range(4):
                            v = jnp.where(masks[q], jnp.where(left[q], jnp.where(ends[q], 0.0, y1), y0), 0.0)
                            carry[b][q] = carry[b][q] + v
                return tuple(tuple(c) for c in carry)

            return lax.fori_loop(0, (pos_ref[row, 2 * GROUP] + 3) // 4, some, carry)

        return lax.fori_loop(0, NS, group, carry)

    carry = tuple((zero,) * 4 for _ in range(1 if last else 2))
    carry = add(-1, (0,), carry)
    carry = add(0, (0,) if last else (0, 1), carry)
    if not last:
        carry = add(1, (1,), carry)
    for block, values in enumerate(carry):
        for q in range(4):
            out_ref[block, :, q * LN : (q + 1) * LN] = values[q]


def illumination(last, pos, probe):
    return pl.pallas_call(
        functools.partial(illum_kernel, last),
        out_shape=jax.ShapeDtypeStruct((1 if last else 2, SR, OW), F32),
        in_specs=[smem(), vmem()],
        out_specs=vmem(),
        scratch_shapes=[pltpu.VMEM((2, PS + 2 * SR, LN), F32)],
        compiler_params=params(),
        name="illumination",
    )(pos, probe)


def step_kernel(last, *refs):
    if last:
        own_ref, up_ref, ill_ref, p0_ref, p1_ref, out_ref = refs
        up = up_ref[...].astype(F32)
    else:
        own_ref, next_ref, inner_ref, outer_ref, ill_ref, p0_ref, p1_ref, out_ref = refs
        odd = odd_tile()
        inner = inner_ref[: 2 * SR, :].astype(F32)
        outer = outer_ref[: 2 * SR, :].astype(F32)
        up = jnp.where(odd, inner, outer)
        down = jnp.where(odd, outer, inner)
    probe = p0_ref[...].astype(F32) + p1_ref[...].astype(F32)
    w = probe[32:] + REG
    parts = []
    for k in range(2):
        a = k * SR
        parts.append((own_ref[a : a + SR, :] + up[a : a + SR, :]) / (ill_ref[0] + REG))
    if last:
        root = jnp.sqrt(w)
        parts += [probe[:16] / root, probe[16:32] / root, root]
    else:
        for k in range(2):
            a = k * SR
            parts.append((next_ref[a : a + SR, :] + down[a : a + SR, :]) / (ill_ref[1] + REG))
        parts += [probe[:16] / w, probe[16:32] / w]
    at = 0
    for part in parts:
        n = part.shape[0]
        part = part.astype(BF)
        for s in range(NS):
            out_ref[s, at : at + n, :] = part
        at += n


def steps(last, *args):
    rows = 2 * SR + 48 if last else 4 * SR + 32
    return pl.pallas_call(
        functools.partial(step_kernel, last),
        out_shape=jax.ShapeDtypeStruct((NS, rows, OW), BF),
        in_specs=[vmem()] * len(args),
        out_specs=vmem(),
        compiler_params=params(),
        name="steps",
    )(*args)


def final_kernel(obj_ref, probe_ref, recv_ref, obj_out, probe_out, grad_out):
    for s in range(NS):
        a = s * SR
        root = recv_ref[s, 2 * SR + 32 : 2 * SR + 48, :].astype(F32)
        for k in range(2):
            obj_out[k, a : a + SR, :] = obj_ref[k, a : a + SR, :] + recv_ref[s, k * SR : (k + 1) * SR, :].astype(F32)
            grad = recv_ref[s, 2 * SR + 16 * k : 2 * SR + 16 * (k + 1), :].astype(F32)
            d = grad / root
            for q in range(2):
                b = a + 16 * q
                grad_out[k, b : b + 16, :] = grad[:, q * PS : (q + 1) * PS]
                probe_out[k, b : b + 16, :] = probe_ref[k, b : b + 16, :] + d[:, q * PS : (q + 1) * PS]


def final(obj, probe, recv):
    return pl.pallas_call(
        final_kernel,
        out_shape=[
            jax.ShapeDtypeStruct((2, TH, OW), F32),
            jax.ShapeDtypeStruct((2, PS, PS), F32),
            jax.ShapeDtypeStruct((2, PS, PS), F32),
        ],
        in_specs=[vmem()] * 3,
        out_specs=[vmem()] * 3,
        compiler_params=params(),
        name="final",
    )(obj, probe, recv)


def shifted(block, distance):
    return lax.ppermute(block, "tile", [(i, i + distance) for i in range(NT) if 0 <= i + distance < NT])


def swapped(block, bits):
    return lax.ppermute(block, "tile", [(i, i ^ bits) for i in range(NT)])


def four(x, swaps):
    y = [swap.astype(F32) for swap in swaps]
    return ((x.astype(F32) + y[0]) + (y[1] + y[2])).astype(BF)


def exchange(blocks):
    return lax.all_to_all(blocks, "scan", 0, 0, tiled=True)


def on_device(object_field, probe, amplitudes, positions, counts):
    tabs = table_arrays()
    pos = positions[0, 0].T
    cnt = counts[0, 0].reshape(1)
    amps = amplitudes[0, 0]
    halo = shifted(object_field.astype(BF), -1)
    live = lax.broadcasted_iota(jnp.int32, (CAP,), 0) < cnt
    row = jnp.concatenate([jnp.where(live, pos[0] - lax.axis_index("tile") * TH + 1, 0), pos[1], cnt])
    mine = lax.broadcasted_iota(jnp.int32, (16, 1), 0) == lax.axis_index("scan")
    posblk = jnp.where(mine, row[None, :], 0).astype(BF)
    posblk = jnp.pad(posblk, ((0, 0), (0, OW - row.shape[0])))
    coded = 2 * GROUP + 1
    (send,) = patterns(pos, cnt, object_field, halo, probe, amps, posblk, tabs)
    own, nxt, part, inner, outer, tile_pos = sums(False, exchange(send))
    swaps = [swapped(part, 1), swapped(part, 2), swapped(part, 3)]
    inner = swapped(inner, 1)
    outer = lax.ppermute(outer, "tile", [(i, i + 1 if i % 2 else i - 1) for i in range(1, NT - 1)])
    part = four(part, swaps)
    swaps = [swapped(part, 4), swapped(part, 8), swapped(part, 12)]
    odd = odd_tile()
    above = jnp.where(odd, inner[2 * SR :, :coded], outer[2 * SR :, :coded])[:NS]
    below = jnp.where(odd, outer[2 * SR :, :coded], inner[2 * SR :, :coded])[:NS]
    around = jnp.concatenate([above.astype(F32), tile_pos[:NS, :coded], below.astype(F32)], 0).astype(jnp.int32)
    ill = illumination(False, around, probe)
    part, ill = lax.optimization_barrier((four(part, swaps), ill))
    other = swapped(part, 16)
    recv = exchange(steps(False, own, nxt, inner, outer, ill, part, other))
    send, object_field, probe = patterns(pos, cnt, object_field, halo, probe, amps, posblk, tabs, recv)
    own, nxt, part, up = sums(True, exchange(send))
    swaps = [swapped(part, 1), swapped(part, 2), swapped(part, 3)]
    up = shifted(up, 1)
    ill = illumination(True, around, probe)
    part, ill = lax.optimization_barrier((four(part, swaps), ill))
    swaps = [swapped(part, 4), swapped(part, 8), swapped(part, 12)]
    part = four(part, swaps)
    other = swapped(part, 16)
    recv = exchange(steps(True, own, up, ill, part, other))
    return tuple(final(object_field, probe, recv))


def solution(mesh):
    in_specs = (
        P(None, "tile", None),
        P(),
        P("scan", "tile", None, None, None),
        P("scan", "tile", None, None),
        P("scan", "tile"),
    )
    out_specs = (P(None, "tile", None), P(), P())
    return jax.shard_map(on_device, mesh=mesh, in_specs=in_specs, out_specs=out_specs, check_vma=False)
```

```python
import functools
import math

import jax
import jax.numpy as jnp
import numpy as np
from jax import lax
from jax.experimental import pallas as pl
from jax.experimental.pallas import tpu as pltpu
from jax.sharding import PartitionSpec as P

ITERS = 2
PS = 256
TH = 256
OW = 512
CAP = 12
NS = 8
NT = 32
SR = TH // NS
LN = 128
PAIR = 3
FLOOR2 = 0.25
REG = 1.0

OWN, NEXT, PRB, POS = 0, 2 * SR, 4 * SR, 4 * SR + 48
SEND = POS + 16
GROUP = 12

BF = jnp.bfloat16
F32 = jnp.float32


def tables():
    n = np.arange(PS, dtype=np.int64)
    angle = ((n[:, None] * n[None, :]) % PS).astype(np.float32) * np.float32(2.0 * math.pi / PS)
    c = (np.cos(angle) / np.sqrt(PS)).astype(np.float32)
    s = (np.sin(angle) / np.sqrt(PS)).astype(np.float32)
    return c, s


def table_arrays():
    c, s = tables()
    return [jnp.asarray(np.block(m).astype(jnp.bfloat16)) for m in ([[c, -s], [s, c]], [[c, s], [-s, c]])]


def pattern_kernel(first, pos_ref, cnt_ref, obj_ref, halo_ref, probe_ref, m1_ref, m2_ref, amp_ref, extra_ref, *rest):
    if first:
        send_ref, x, pr, g, pg, patch, h, h2, amp, m1, m2, low, send, extra, sems, amp_sems, out_sems = rest
    else:
        send_ref, objn_ref, probn_ref, x, pr, g, pg, patch, h, h2, amp, m1, m2, low, send, extra, sems, amp_sems, out_sems = rest
    count = cnt_ref[0]
    lane_blocks = [slice(q * LN, (q + 1) * LN) for q in range(4)]
    ins = [(extra_ref, extra), (probe_ref, pr), (halo_ref, low)]
    ins += [(obj_ref.at[k, :, lane_blocks[q]], x.at[k, q, pl.ds(0, TH), :]) for k in range(2) for q in range(4)]
    ins += [(m1_ref, m1), (m2_ref, m2)]
    ins = [pltpu.make_async_copy(src, dst, sems.at[n]) for n, (src, dst) in enumerate(ins)]
    for copy in ins:
        copy.start()

    def amp_copy(j):
        return pltpu.make_async_copy(amp_ref.at[j], amp.at[j], amp_sems.at[j])

    for j in range(PAIR):
        amp_copy(j).start()
    tile_start = lax.axis_index("tile") * TH
    g[...] = jnp.zeros_like(g)
    pg[...] = jnp.zeros_like(pg)
    for copy in ins[:-2]:
        copy.wait()
    outs = []
    if first:
        for q in range(4):
            x[:, q, TH:, :] = low[:, :, lane_blocks[q]].astype(F32)
    else:
        for s in range(NS):
            for k in range(2):
                a = s * SR
                d = extra[s, k * SR : (k + 1) * SR, :].astype(F32)
                e = low[k, a : a + SR, :].astype(F32) + extra[s, (2 + k) * SR : (3 + k) * SR, :].astype(F32)
                for q in range(4):
                    x[k, q, a : a + SR, :] += d[:, lane_blocks[q]]
                    x[k, q, TH + a : TH + a + SR, :] = e[:, lane_blocks[q]]
                d = extra[s, 4 * SR + 16 * k : 4 * SR + 16 * (k + 1), :].astype(F32)
                for q in range(2):
                    b = a + 16 * q
                    pr[k, b : b + 16, :] += d[:, q * PS : (q + 1) * PS]
        outs += [(x.at[k, q, pl.ds(0, TH), :], objn_ref.at[k, :, lane_blocks[q]]) for k in range(2) for q in range(4)]
        outs += [(pr, probn_ref)]
    outs = [pltpu.make_async_copy(src, dst, out_sems.at[n]) for n, (src, dst) in enumerate(outs)]
    for copy in outs:
        copy.start()

    def place(j):
        r = pos_ref[0, j] - tile_start
        c = pos_ref[1, j]
        base = jnp.where(c >= LN, 1, 0)
        return r, base, c - base * LN

    lanes = lax.broadcasted_iota(jnp.int32, (PS, LN), 1)

    def to_half(j, slot, live):
        r, base, off = place(j)
        head = lanes < LN - off
        turn = (LN - off) & (LN - 1)
        xs = []
        for k in range(2):
            v = [pltpu.roll(x[k, base + q, pl.ds(r, PS), :], turn, 1) for q in range(3)]
            v = jnp.concatenate([jnp.where(head, v[0], v[1]), jnp.where(head, v[1], v[2])], 1)
            patch[slot, k] = v
            xs.append(v)
        xr, xi = xs
        p0, p1 = pr[0], pr[1]
        pg[2] += (xr * xr + xi * xi) * live
        w = jnp.concatenate([(p0 * xr - p1 * xi).astype(BF), (p0 * xi + p1 * xr).astype(BF)], 1)
        half = jnp.dot(w, m1[...], preferred_element_type=F32).astype(BF)
        h[slot, :PS, :] = half[:, :PS]
        h[slot, PS:, :] = half[:, PS:]

    def to_back_half(j, slot, live):
        far = jnp.dot(m2[...], h[slot], preferred_element_type=F32)
        fr, fi = far[:PS], far[PS:]
        m = jnp.maximum(fr * fr + fi * fi, FLOOR2)
        q = amp[j].astype(F32) * lax.rsqrt(m) - 1.0
        q = q * live
        u = jnp.concatenate([(q * fr).astype(BF), (q * fi).astype(BF)], 1)
        half = jnp.dot(u, m2[...], preferred_element_type=F32).astype(BF)
        h2[slot, :PS, :] = half[:, :PS]
        h2[slot, PS:, :] = half[:, PS:]

    def add_back(j, slot):
        back = jnp.dot(m1[...], h2[slot], preferred_element_type=F32)
        br, bi = back[:PS], back[PS:]
        xr, xi = patch[slot, 0], patch[slot, 1]
        pg[0] += xr * br + xi * bi
        pg[1] += xr * bi - xi * br
        p0, p1 = pr[0], pr[1]
        r, base, off = place(j)
        tail = lanes >= off
        turn = off & (LN - 1)
        for k, o in enumerate((p0 * br + p1 * bi, p0 * bi - p1 * br)):
            v = [pltpu.roll(o[:, q * LN : (q + 1) * LN], turn, 1) for q in range(2)]
            g[k, base, pl.ds(r, PS), :] += jnp.where(tail, v[0], 0.0)
            g[k, base + 1, pl.ds(r, PS), :] += jnp.where(tail, v[1], v[0])
            g[k, base + 2, pl.ds(r, PS), :] += jnp.where(tail, 0.0, v[1])

    for copy in ins[-2:]:
        copy.wait()

    def visit(i, carry):
        j = [PAIR * i + n for n in range(PAIR)]
        live = [jnp.where(n < count, 1.0, 0.0) for n in j]
        for n in range(PAIR):
            amp_copy(j[n]).wait()

        @pl.when(i + 1 < visits)
        def _():
            for n in range(PAIR):
                amp_copy(j[n] + PAIR).start()

        for n in range(PAIR):
            to_half(j[n], n, live[n])
        for n in range(PAIR):
            to_back_half(j[n], n, live[n])
        for n in range(PAIR):
            add_back(j[n], n)
        return carry

    visits = jnp.clip((count + PAIR - 1) // PAIR, 1, CAP // PAIR)
    lax.fori_loop(0, visits, visit, 0)
    for s in range(NS):
        a = s * SR
        for k in range(2):
            for q in range(4):
                send[s, OWN + k * SR : OWN + (k + 1) * SR, lane_blocks[q]] = g[k, q, a : a + SR, :].astype(BF)
                send[s, NEXT + k * SR : NEXT + (k + 1) * SR, lane_blocks[q]] = g[k, q, TH + a : TH + a + SR, :].astype(BF)
        for k in range(3):
            send[s, PRB + 16 * k : PRB + 16 * (k + 1), :] = jnp.concatenate(
                [pg[k, a : a + 16, :], pg[k, a + 16 : a + 32, :]], 1
            ).astype(BF)
        if first:
            send[s, POS:, :] = extra[...]
        copy = pltpu.make_async_copy(send.at[s], send_ref.at[s], out_sems.at[len(outs)])
        copy.start()
        outs.append(copy)
    for copy in outs:
        copy.wait()


def smem():
    return pl.BlockSpec(memory_space=pltpu.SMEM)


def vmem():
    return pl.BlockSpec(memory_space=pltpu.VMEM)


def anywhere():
    return pl.BlockSpec(memory_space=pl.ANY)


def params(mib):
    return pltpu.CompilerParams(vmem_limit_bytes=mib * 1024 * 1024)


def patterns(pos, cnt, obj, halo, probe, amps, tabs, posblk=None, recv=None):
    first = recv is None
    rows = SEND if first else POS
    out = [jax.ShapeDtypeStruct((NS, rows, OW), BF)]
    if not first:
        out += [jax.ShapeDtypeStruct((2, TH, OW), F32), jax.ShapeDtypeStruct((2, PS, PS), F32)]
    extra = posblk if first else recv
    args = [pos, cnt, obj, halo, probe, *tabs, amps, extra]
    return pl.pallas_call(
        functools.partial(pattern_kernel, first),
        out_shape=out,
        in_specs=[smem(), smem()] + [anywhere()] * (len(args) - 2),
        out_specs=[anywhere()] * len(out),
        scratch_shapes=[
            pltpu.VMEM((2, 4, 2 * TH, LN), F32),
            pltpu.VMEM((2, PS, PS), F32),
            pltpu.VMEM((2, 4, 2 * TH, LN), F32),
            pltpu.VMEM((3, PS, PS), F32),
            pltpu.VMEM((PAIR, 2, PS, PS), F32),
            pltpu.VMEM((PAIR, 2 * PS, PS), BF),
            pltpu.VMEM((PAIR, 2 * PS, PS), BF),
            pltpu.VMEM((CAP, PS, PS), BF),
            pltpu.VMEM((2 * PS, 2 * PS), BF),
            pltpu.VMEM((2 * PS, 2 * PS), BF),
            pltpu.VMEM((2, TH, OW), BF),
            pltpu.VMEM((NS, rows, OW), BF),
            pltpu.VMEM(extra.shape, BF),
            pltpu.SemaphoreType.DMA((13,)),
            pltpu.SemaphoreType.DMA((CAP,)),
            pltpu.SemaphoreType.DMA((9 + NS,)),
        ],
        compiler_params=params(48),
        name="patterns",
    )(*args)


def sum_kernel(last, recv_ref, own_ref, probe_ref, up_ref, *rest):
    *pos_ref, recv, sems = rest
    copies = [pltpu.make_async_copy(recv_ref.at[s], recv.at[s], sems.at[s]) for s in range(NS)]
    for copy in copies:
        copy.start()
    for copy in copies:
        copy.wait()

    def total(a, n):
        t = [recv[s, a : a + n, :].astype(F32) for s in range(NS)]
        return ((t[0] + t[1]) + (t[2] + t[3])) + ((t[4] + t[5]) + (t[6] + t[7]))

    probe_ref[...] = total(PRB, 48).astype(BF)
    own_ref[...] = total(OWN, 2 * SR)
    up_ref[: 2 * SR, :] = total(NEXT, 2 * SR).astype(BF)
    if not last:
        pos = total(POS, 16)
        pos_ref[0][...] = pos[:, :LN]
        up_ref[2 * SR :, :] = pos.astype(BF)


def sums(last, recv):
    out = [jax.ShapeDtypeStruct((2 * SR, OW), F32), jax.ShapeDtypeStruct((48, OW), BF)]
    if last:
        out += [jax.ShapeDtypeStruct((2 * SR, OW), BF)]
    else:
        out += [jax.ShapeDtypeStruct((2 * SR + 16, OW), BF), jax.ShapeDtypeStruct((16, LN), F32)]
    return pl.pallas_call(
        functools.partial(sum_kernel, last),
        out_shape=out,
        in_specs=[anywhere()],
        out_specs=[vmem()] * len(out),
        scratch_shapes=[pltpu.VMEM(recv.shape, BF), pltpu.SemaphoreType.DMA((NS,))],
        compiler_params=params(8),
        name="sums",
    )(recv)


def own_kernel(pos_ref, probe_ref, own_ref, up_ref, out_ref, p2):
    for q in range(2):
        cols = slice(q * LN, (q + 1) * LN)
        p2[q, :SR, :] = jnp.zeros((SR, LN), F32)
        p2[q, SR + PS :, :] = jnp.zeros((SR, LN), F32)
        p2[q, SR : SR + PS, :] = probe_ref[0, :, cols] * probe_ref[0, :, cols] + probe_ref[1, :, cols] * probe_ref[1, :, cols]
    mine = lax.axis_index("scan") * SR
    lanes = lax.broadcasted_iota(jnp.int32, (8, LN), 1)
    parts = SR // 8

    def group(row, carry):
        shift = jnp.where(row < NS, -TH, 0) - 1

        def some(i, carry):
            carry = [list(c) for c in carry]
            for n in range(4):
                code = pos_ref[row, 4 * i + n]
                start = jnp.where(code > 0, code + shift, -4 * TH)
                c = pos_ref[row, GROUP + 4 * i + n]
                far = c >= LN
                off = jnp.where(far, c - LN, c)
                tail = lanes >= off
                turn = off & (LN - 1)
                at = jnp.clip(mine - start, -SR, PS) + SR
                for b in range(parts):
                    y0, y1 = (pltpu.roll(p2[q, pl.ds(at + 8 * b, 8), :], turn, 1) for q in range(2))
                    v = (0.0, jnp.where(tail, y0, 0.0), jnp.where(tail, y1, y0), jnp.where(tail, 0.0, y1), 0.0)
                    for q in range(4):
                        carry[b][q] = carry[b][q] + jnp.where(far, v[q], v[q + 1])
            return tuple(tuple(c) for c in carry)

        return lax.fori_loop(0, (pos_ref[row, 2 * GROUP] + 3) // 4, some, carry)

    zero = jnp.zeros((8, LN), F32)
    carry = lax.fori_loop(0, 2 * NS, group, ((zero,) * 4,) * parts)
    for q in range(4):
        cols = slice(q * LN, (q + 1) * LN)
        scale = 1.0 / (jnp.concatenate([carry[b][q] for b in range(parts)], 0) + REG)
        for k in range(2):
            a = k * SR
            out_ref[a : a + SR, cols] = ((own_ref[a : a + SR, cols] + up_ref[a : a + SR, cols].astype(F32)) * scale).astype(BF)


def own_step(pos, probe, own, up):
    return pl.pallas_call(
        own_kernel,
        out_shape=jax.ShapeDtypeStruct((2 * SR, OW), BF),
        in_specs=[smem(), vmem(), vmem(), vmem()],
        out_specs=vmem(),
        scratch_shapes=[pltpu.VMEM((2, PS + 2 * SR, LN), F32)],
        compiler_params=params(8),
        name="own_step",
    )(pos, probe, own, up)


def spread_kernel(last, *refs):
    *deltas, p0_ref, p1_ref, out_ref, block, sems = refs
    probe = p0_ref[...].astype(F32) + p1_ref[...].astype(F32)
    w = probe[32:] + REG
    at = 0
    for delta in deltas:
        block[at : at + 2 * SR, :] = delta[...]
        at += 2 * SR
    if last:
        root = jnp.sqrt(w)
        parts = [probe[:16] / root, probe[16:32] / root, root]
    else:
        parts = [probe[:16] / w, probe[16:32] / w]
    for part in parts:
        block[at : at + 16, :] = part.astype(BF)
        at += 16
    copies = [pltpu.make_async_copy(block, out_ref.at[s], sems.at[s]) for s in range(NS)]
    for copy in copies:
        copy.start()
    for copy in copies:
        copy.wait()


def spread(last, *args):
    rows = 2 * SR + 48 if last else 4 * SR + 32
    return pl.pallas_call(
        functools.partial(spread_kernel, last),
        out_shape=jax.ShapeDtypeStruct((NS, rows, OW), BF),
        in_specs=[vmem()] * len(args),
        out_specs=anywhere(),
        scratch_shapes=[pltpu.VMEM((rows, OW), BF), pltpu.SemaphoreType.DMA((NS,))],
        compiler_params=params(8),
        name="spread",
    )(*args)


def final_kernel(obj_ref, probe_ref, recv_ref, obj_out, probe_out, grad_out, obj, probe, recv, grad, sems, out_sems):
    ins = []
    for s in range(NS):
        rows = pl.ds(s * SR, SR)
        pairs = [(recv_ref.at[s], recv.at[s]), (obj_ref.at[:, rows, :], obj.at[:, rows, :])]
        pairs += [(probe_ref.at[:, rows, :], probe.at[:, rows, :])]
        ins.append([pltpu.make_async_copy(src, dst, sems.at[s, n]) for n, (src, dst) in enumerate(pairs)])
    for copies in ins:
        for copy in copies:
            copy.start()
    outs = []
    for s in range(NS):
        for copy in ins[s]:
            copy.wait()
        a = s * SR
        root = recv[s, 2 * SR + 32 : 2 * SR + 48, :].astype(F32)
        for k in range(2):
            obj[k, a : a + SR, :] += recv[s, k * SR : (k + 1) * SR, :].astype(F32)
            top = recv[s, 2 * SR + 16 * k : 2 * SR + 16 * (k + 1), :].astype(F32)
            d = top / root
            for q in range(2):
                b = a + 16 * q
                grad[k, b : b + 16, :] = top[:, q * PS : (q + 1) * PS]
                probe[k, b : b + 16, :] += d[:, q * PS : (q + 1) * PS]
        rows = pl.ds(a, SR)
        pairs = [(obj, obj_out), (probe, probe_out), (grad, grad_out)]
        for n, (src, dst) in enumerate(pairs):
            copy = pltpu.make_async_copy(src.at[:, rows, :], dst.at[:, rows, :], out_sems.at[s, n])
            copy.start()
            outs.append(copy)
    for copy in outs:
        copy.wait()


def final(obj, probe, recv):
    return pl.pallas_call(
        final_kernel,
        out_shape=[
            jax.ShapeDtypeStruct((2, TH, OW), F32),
            jax.ShapeDtypeStruct((2, PS, PS), F32),
            jax.ShapeDtypeStruct((2, PS, PS), F32),
        ],
        in_specs=[anywhere()] * 3,
        out_specs=[anywhere()] * 3,
        scratch_shapes=[
            pltpu.VMEM((2, TH, OW), F32),
            pltpu.VMEM((2, PS, PS), F32),
            pltpu.VMEM(recv.shape, BF),
            pltpu.VMEM((2, PS, PS), F32),
            pltpu.SemaphoreType.DMA((NS, 3)),
            pltpu.SemaphoreType.DMA((NS, 3)),
        ],
        compiler_params=params(16),
        name="final",
    )(obj, probe, recv)


def shifted(block, distance):
    return lax.ppermute(block, "tile", [(i, i + distance) for i in range(NT) if 0 <= i + distance < NT])


def swapped(block, bits):
    return lax.ppermute(block, "tile", [(i, i ^ bits) for i in range(NT)])


def four(x, swaps):
    y = [swap.astype(F32) for swap in swaps]
    return ((x.astype(F32) + y[0]) + (y[1] + y[2])).astype(BF)


def exchange(blocks):
    return lax.all_to_all(blocks, "scan", 0, 0, tiled=True)


def on_device(object_field, probe, amplitudes, positions, counts):
    tabs = table_arrays()
    pos = positions[0, 0].T
    cnt = counts[0, 0].reshape(1)
    amps = amplitudes[0, 0]
    halo = shifted(object_field.astype(BF), -1)
    live = lax.broadcasted_iota(jnp.int32, (CAP,), 0) < cnt
    row = jnp.concatenate([jnp.where(live, pos[0] - lax.axis_index("tile") * TH + 1, 0), pos[1], cnt])
    mine = lax.broadcasted_iota(jnp.int32, (16, 1), 0) == lax.axis_index("scan")
    posblk = jnp.where(mine, row[None, :], 0).astype(BF)
    posblk = jnp.pad(posblk, ((0, 0), (0, OW - row.shape[0])))
    coded = 2 * GROUP + 1
    (send,) = patterns(pos, cnt, object_field, halo, probe, amps, tabs, posblk=posblk)
    own, part, up, tile_pos = sums(False, exchange(send))
    swaps = [swapped(part, 1), swapped(part, 2), swapped(part, 3)]
    up = shifted(up, 1)
    part = four(part, swaps)
    swaps = [swapped(part, 4), swapped(part, 8), swapped(part, 12)]
    around = jnp.concatenate([up[2 * SR :, :coded][:NS].astype(F32), tile_pos[:NS, :coded]], 0).astype(jnp.int32)
    delta = own_step(around, probe, own, up)
    part, delta = lax.optimization_barrier((four(part, swaps), delta))
    other = swapped(part, 16)
    recv = exchange(spread(False, delta, shifted(delta, -1), part, other))
    send, object_field, probe = patterns(pos, cnt, object_field, halo, probe, amps, tabs, recv=recv)
    own, part, up = sums(True, exchange(send))
    swaps = [swapped(part, 1), swapped(part, 2), swapped(part, 3)]
    up = shifted(up, 1)
    part = four(part, swaps)
    swaps = [swapped(part, 4), swapped(part, 8), swapped(part, 12)]
    delta = own_step(around, probe, own, up)
    part, delta = lax.optimization_barrier((four(part, swaps), delta))
    other = swapped(part, 16)
    recv = exchange(spread(True, delta, part, other))
    return tuple(final(object_field, probe, recv))


def solution(mesh):
    in_specs = (
        P(None, "tile", None),
        P(),
        P("scan", "tile", None, None, None),
        P("scan", "tile", None, None),
        P("scan", "tile"),
    )
    out_specs = (P(None, "tile", None), P(), P())
    return jax.shard_map(on_device, mesh=mesh, in_specs=in_specs, out_specs=out_specs, check_vma=False)
```

```python
import functools
import math

import jax
import jax.numpy as jnp
import numpy as np
from jax import lax
from jax.experimental import pallas as pl
from jax.experimental.pallas import tpu as pltpu
from jax.sharding import PartitionSpec as P

ITERS = 2
PS = 256
TH = 256
OW = 512
CAP = 12
NS = 8
NT = 32
SR = TH // NS
LN = 128
GRANT = 20
PAIR = 3
FLOOR2 = 0.25
REG = 1.0

OWN, NEXT, PRB, POS = 0, 2 * SR, 4 * SR, 4 * SR + 48
SEND = POS + 16
GROUP = 12

BF = jnp.bfloat16
F32 = jnp.float32


def tables():
    n = np.arange(PS, dtype=np.int64)
    angle = ((n[:, None] * n[None, :]) % PS).astype(np.float32) * np.float32(2.0 * math.pi / PS)
    c = (np.cos(angle) / np.sqrt(PS)).astype(np.float32)
    s = (np.sin(angle) / np.sqrt(PS)).astype(np.float32)
    return c, s


def table_arrays():
    c, s = tables()
    return [jnp.asarray(np.block(m).astype(jnp.bfloat16)) for m in ([[c, -s], [s, c]], [[c, s], [-s, c]])]


def pattern_kernel(first, pos_ref, cnt_ref, obj_ref, halo_ref, probe_ref, amp_ref, extra_ref, m1, m2, *rest):
    if first:
        send, x, g, pg, patch, h, h2 = rest
        pr = probe_ref
    else:
        send, objn_ref, pr, x, g, pg, patch, h, h2 = rest
    count = cnt_ref[0]
    lane_blocks = [slice(q * LN, (q + 1) * LN) for q in range(4)]
    tile_start = lax.axis_index("tile") * TH
    g[...] = jnp.zeros_like(g)
    pg[...] = jnp.zeros_like(pg)
    if first:
        for q in range(4):
            x[:, q, :TH, :] = obj_ref[:, :, lane_blocks[q]]
            x[:, q, TH:, :] = halo_ref[:, :, lane_blocks[q]].astype(F32)
    else:
        for s in range(NS):
            for k in range(2):
                a = s * SR
                d = obj_ref[k, a : a + SR, :] + extra_ref[s, k * SR : (k + 1) * SR, :].astype(F32)
                e = halo_ref[k, a : a + SR, :].astype(F32) + extra_ref[s, (2 + k) * SR : (3 + k) * SR, :].astype(F32)
                objn_ref[k, a : a + SR, :] = d
                for q in range(4):
                    x[k, q, a : a + SR, :] = d[:, lane_blocks[q]]
                    x[k, q, TH + a : TH + a + SR, :] = e[:, lane_blocks[q]]
                d = extra_ref[s, 4 * SR + 16 * k : 4 * SR + 16 * (k + 1), :].astype(F32)
                for q in range(2):
                    b = a + 16 * q
                    pr[k, b : b + 16, :] = probe_ref[k, b : b + 16, :] + d[:, q * PS : (q + 1) * PS]

    def place(j):
        r = pos_ref[0, j] - tile_start
        c = pos_ref[1, j]
        base = jnp.where(c >= LN, 1, 0)
        return r, base, c - base * LN

    lanes = lax.broadcasted_iota(jnp.int32, (PS, LN), 1)

    def to_half(j, slot, live):
        r, base, off = place(j)
        head = lanes < LN - off
        turn = (LN - off) & (LN - 1)
        xs = []
        for k in range(2):
            v = [pltpu.roll(x[k, base + q, pl.ds(r, PS), :], turn, 1) for q in range(3)]
            v = jnp.concatenate([jnp.where(head, v[0], v[1]), jnp.where(head, v[1], v[2])], 1)
            patch[slot, k] = v
            xs.append(v)
        xr, xi = xs
        p0, p1 = pr[0], pr[1]
        pg[2] += (xr * xr + xi * xi) * live
        w = jnp.concatenate([(p0 * xr - p1 * xi).astype(BF), (p0 * xi + p1 * xr).astype(BF)], 1)
        half = jnp.dot(w, m1[...], preferred_element_type=F32).astype(BF)
        h[slot, :PS, :] = half[:, :PS]
        h[slot, PS:, :] = half[:, PS:]

    def to_back_half(j, slot, live):
        far = jnp.dot(m2[...], h[slot], preferred_element_type=F32)
        fr, fi = far[:PS], far[PS:]
        m = jnp.maximum(fr * fr + fi * fi, FLOOR2)
        q = amp_ref[j].astype(F32) * lax.rsqrt(m) - 1.0
        q = q * live
        u = jnp.concatenate([(q * fr).astype(BF), (q * fi).astype(BF)], 1)
        half = jnp.dot(u, m2[...], preferred_element_type=F32).astype(BF)
        h2[slot, :PS, :] = half[:, :PS]
        h2[slot, PS:, :] = half[:, PS:]

    def add_back(j, slot):
        back = jnp.dot(m1[...], h2[slot], preferred_element_type=F32)
        br, bi = back[:PS], back[PS:]
        xr, xi = patch[slot, 0], patch[slot, 1]
        pg[0] += xr * br + xi * bi
        pg[1] += xr * bi - xi * br
        p0, p1 = pr[0], pr[1]
        r, base, off = place(j)
        tail = lanes >= off
        turn = off & (LN - 1)
        for k, o in enumerate((p0 * br + p1 * bi, p0 * bi - p1 * br)):
            v = [pltpu.roll(o[:, q * LN : (q + 1) * LN], turn, 1) for q in range(2)]
            g[k, base, pl.ds(r, PS), :] += jnp.where(tail, v[0], 0.0)
            g[k, base + 1, pl.ds(r, PS), :] += jnp.where(tail, v[1], v[0])
            g[k, base + 2, pl.ds(r, PS), :] += jnp.where(tail, 0.0, v[1])

    def visit(i, carry):
        j = [PAIR * i + n for n in range(PAIR)]
        live = [jnp.where(n < count, 1.0, 0.0) for n in j]
        for n in range(PAIR):
            to_half(j[n], n, live[n])
        for n in range(PAIR):
            to_back_half(j[n], n, live[n])
        for n in range(PAIR):
            add_back(j[n], n)
        return carry

    lax.fori_loop(0, jnp.minimum((count + PAIR - 1) // PAIR, CAP // PAIR), visit, 0)
    for s in range(NS):
        a = s * SR
        for k in range(2):
            for q in range(4):
                send[s, OWN + k * SR : OWN + (k + 1) * SR, lane_blocks[q]] = g[k, q, a : a + SR, :].astype(BF)
                send[s, NEXT + k * SR : NEXT + (k + 1) * SR, lane_blocks[q]] = g[k, q, TH + a : TH + a + SR, :].astype(BF)
        for k in range(3):
            send[s, PRB + 16 * k : PRB + 16 * (k + 1), :] = jnp.concatenate(
                [pg[k, a : a + 16, :], pg[k, a + 16 : a + 32, :]], 1
            ).astype(BF)
        if first:
            send[s, POS:, :] = extra_ref[...]


def smem():
    return pl.BlockSpec(memory_space=pltpu.SMEM)


def vmem():
    return pl.BlockSpec(memory_space=pltpu.VMEM)


def params(mib):
    return pltpu.CompilerParams(vmem_limit_bytes=mib * 1024 * 1024)


def patterns(pos, cnt, obj, halo, probe, amps, tabs, posblk=None, recv=None):
    first = recv is None
    out = [jax.ShapeDtypeStruct((NS, SEND if first else POS, OW), BF)]
    if not first:
        out += [jax.ShapeDtypeStruct((2, TH, OW), F32), jax.ShapeDtypeStruct((2, PS, PS), F32)]
    args = [pos, cnt, obj, halo, probe, amps, posblk if first else recv, *tabs]
    return pl.pallas_call(
        functools.partial(pattern_kernel, first),
        out_shape=out,
        in_specs=[smem(), smem()] + [vmem()] * 7,
        out_specs=[vmem()] * len(out),
        scratch_shapes=[
            pltpu.VMEM((2, 4, 2 * TH, LN), F32),
            pltpu.VMEM((2, 4, 2 * TH, LN), F32),
            pltpu.VMEM((3, PS, PS), F32),
            pltpu.VMEM((PAIR, 2, PS, PS), F32),
            pltpu.VMEM((PAIR, 2 * PS, PS), BF),
            pltpu.VMEM((PAIR, 2 * PS, PS), BF),
        ],
        compiler_params=params(GRANT),
        name="patterns",
    )(*args)


def sum_kernel(last, recv_ref, own_ref, probe_ref, up_ref, *rest):
    def total(a, n):
        t = [recv_ref[s, a : a + n, :].astype(F32) for s in range(NS)]
        return ((t[0] + t[1]) + (t[2] + t[3])) + ((t[4] + t[5]) + (t[6] + t[7]))

    probe_ref[...] = total(PRB, 48).astype(BF)
    own_ref[...] = total(OWN, 2 * SR)
    up_ref[: 2 * SR, :] = total(NEXT, 2 * SR).astype(BF)
    if not last:
        pos = total(POS, 16)
        rest[0][...] = pos[:, :LN]
        up_ref[2 * SR :, :] = pos.astype(BF)


def sums(last, recv):
    out = [jax.ShapeDtypeStruct((2 * SR, OW), F32), jax.ShapeDtypeStruct((48, OW), BF)]
    if last:
        out += [jax.ShapeDtypeStruct((2 * SR, OW), BF)]
    else:
        out += [jax.ShapeDtypeStruct((2 * SR + 16, OW), BF), jax.ShapeDtypeStruct((16, LN), F32)]
    return pl.pallas_call(
        functools.partial(sum_kernel, last),
        out_shape=out,
        in_specs=[vmem()],
        out_specs=[vmem()] * len(out),
        compiler_params=params(8),
        name="sums",
    )(recv)


def own_kernel(pos_ref, probe_ref, own_ref, up_ref, out_ref, p2):
    for q in range(2):
        cols = slice(q * LN, (q + 1) * LN)
        p2[q, :SR, :] = jnp.zeros((SR, LN), F32)
        p2[q, SR + PS :, :] = jnp.zeros((SR, LN), F32)
        p2[q, SR : SR + PS, :] = probe_ref[0, :, cols] * probe_ref[0, :, cols] + probe_ref[1, :, cols] * probe_ref[1, :, cols]
    mine = lax.axis_index("scan") * SR
    lanes = lax.broadcasted_iota(jnp.int32, (8, LN), 1)
    parts = SR // 8

    def group(row, carry):
        shift = jnp.where(row < NS, -TH, 0) - 1

        def some(i, carry):
            carry = [list(c) for c in carry]
            for n in range(4):
                code = pos_ref[row, 4 * i + n]
                start = jnp.where(code > 0, code + shift, -4 * TH)
                c = pos_ref[row, GROUP + 4 * i + n]
                far = c >= LN
                off = jnp.where(far, c - LN, c)
                tail = lanes >= off
                turn = off & (LN - 1)
                at = jnp.clip(mine - start, -SR, PS) + SR
                for b in range(parts):
                    y0, y1 = (pltpu.roll(p2[q, pl.ds(at + 8 * b, 8), :], turn, 1) for q in range(2))
                    v = (0.0, jnp.where(tail, y0, 0.0), jnp.where(tail, y1, y0), jnp.where(tail, 0.0, y1), 0.0)
                    for q in range(4):
                        carry[b][q] = carry[b][q] + jnp.where(far, v[q], v[q + 1])
            return tuple(tuple(c) for c in carry)

        return lax.fori_loop(0, (pos_ref[row, 2 * GROUP] + 3) // 4, some, carry)

    zero = jnp.zeros((8, LN), F32)
    carry = lax.fori_loop(0, 2 * NS, group, ((zero,) * 4,) * parts)
    for q in range(4):
        cols = slice(q * LN, (q + 1) * LN)
        scale = 1.0 / (jnp.concatenate([carry[b][q] for b in range(parts)], 0) + REG)
        for k in range(2):
            a = k * SR
            out_ref[a : a + SR, cols] = ((own_ref[a : a + SR, cols] + up_ref[a : a + SR, cols].astype(F32)) * scale).astype(BF)


def own_step(pos, probe, own, up):
    return pl.pallas_call(
        own_kernel,
        out_shape=jax.ShapeDtypeStruct((2 * SR, OW), BF),
        in_specs=[smem(), vmem(), vmem(), vmem()],
        out_specs=vmem(),
        scratch_shapes=[pltpu.VMEM((2, PS + 2 * SR, LN), F32)],
        compiler_params=params(8),
        name="own_step",
    )(pos, probe, own, up)


def spread_kernel(last, *refs):
    *deltas, p0_ref, p1_ref, out_ref = refs
    probe = p0_ref[...].astype(F32) + p1_ref[...].astype(F32)
    w = probe[32:] + REG
    parts = [delta[...] for delta in deltas]
    if last:
        root = jnp.sqrt(w)
        parts += [probe[:16] / root, probe[16:32] / root, root]
    else:
        parts += [probe[:16] / w, probe[16:32] / w]
    at = 0
    for part in parts:
        n = part.shape[0]
        for s in range(NS):
            out_ref[s, at : at + n, :] = part.astype(BF)
        at += n


def spread(last, *args):
    rows = 2 * SR + 48 if last else 4 * SR + 32
    return pl.pallas_call(
        functools.partial(spread_kernel, last),
        out_shape=jax.ShapeDtypeStruct((NS, rows, OW), BF),
        in_specs=[vmem()] * len(args),
        out_specs=vmem(),
        compiler_params=params(8),
        name="spread",
    )(*args)


def final_kernel(obj_ref, probe_ref, recv_ref, obj_out, probe_out, grad_out):
    for s in range(NS):
        a = s * SR
        root = recv_ref[s, 2 * SR + 32 : 2 * SR + 48, :].astype(F32)
        for k in range(2):
            obj_out[k, a : a + SR, :] = obj_ref[k, a : a + SR, :] + recv_ref[s, k * SR : (k + 1) * SR, :].astype(F32)
            grad = recv_ref[s, 2 * SR + 16 * k : 2 * SR + 16 * (k + 1), :].astype(F32)
            d = grad / root
            for q in range(2):
                b = a + 16 * q
                grad_out[k, b : b + 16, :] = grad[:, q * PS : (q + 1) * PS]
                probe_out[k, b : b + 16, :] = probe_ref[k, b : b + 16, :] + d[:, q * PS : (q + 1) * PS]


def final(obj, probe, recv):
    return pl.pallas_call(
        final_kernel,
        out_shape=[
            jax.ShapeDtypeStruct((2, TH, OW), F32),
            jax.ShapeDtypeStruct((2, PS, PS), F32),
            jax.ShapeDtypeStruct((2, PS, PS), F32),
        ],
        in_specs=[vmem()] * 3,
        out_specs=[vmem()] * 3,
        compiler_params=params(8),
        name="final",
    )(obj, probe, recv)


def shifted(block, distance):
    return lax.ppermute(block, "tile", [(i, i + distance) for i in range(NT) if 0 <= i + distance < NT])


def swapped(block, bits):
    return lax.ppermute(block, "tile", [(i, i ^ bits) for i in range(NT)])


def four(x, swaps):
    y = [swap.astype(F32) for swap in swaps]
    return ((x.astype(F32) + y[0]) + (y[1] + y[2])).astype(BF)


def exchange(blocks):
    return lax.all_to_all(blocks, "scan", 0, 0, tiled=True)


def on_device(object_field, probe, amplitudes, positions, counts):
    tabs = table_arrays()
    pos = positions[0, 0].T
    cnt = counts[0, 0].reshape(1)
    amps = amplitudes[0, 0]
    halo = shifted(object_field.astype(BF), -1)
    live = lax.broadcasted_iota(jnp.int32, (CAP,), 0) < cnt
    row = jnp.concatenate([jnp.where(live, pos[0] - lax.axis_index("tile") * TH + 1, 0), pos[1], cnt])
    mine = lax.broadcasted_iota(jnp.int32, (16, 1), 0) == lax.axis_index("scan")
    posblk = jnp.where(mine, row[None, :], 0).astype(BF)
    posblk = jnp.pad(posblk, ((0, 0), (0, OW - row.shape[0])))
    coded = 2 * GROUP + 1
    (send,) = patterns(pos, cnt, object_field, halo, probe, amps, tabs, posblk=posblk)
    own, part, up, tile_pos = sums(False, exchange(send))
    swaps = [swapped(part, 1), swapped(part, 2), swapped(part, 3)]
    up = shifted(up, 1)
    part = four(part, swaps)
    swaps = [swapped(part, 4), swapped(part, 8), swapped(part, 12)]
    around = jnp.concatenate([up[2 * SR :, :coded][:NS].astype(F32), tile_pos[:NS, :coded]], 0).astype(jnp.int32)
    delta = own_step(around, probe, own, up)
    part, delta = lax.optimization_barrier((four(part, swaps), delta))
    other = swapped(part, 16)
    recv = exchange(spread(False, delta, shifted(delta, -1), part, other))
    send, object_field, probe = patterns(pos, cnt, object_field, halo, probe, amps, tabs, recv=recv)
    own, part, up = sums(True, exchange(send))
    swaps = [swapped(part, 1), swapped(part, 2), swapped(part, 3)]
    up = shifted(up, 1)
    part = four(part, swaps)
    swaps = [swapped(part, 4), swapped(part, 8), swapped(part, 12)]
    delta = own_step(around, probe, own, up)
    part, delta = lax.optimization_barrier((four(part, swaps), delta))
    other = swapped(part, 16)
    recv = exchange(spread(True, delta, part, other))
    return tuple(final(object_field, probe, recv))


def solution(mesh):
    in_specs = (
        P(None, "tile", None),
        P(),
        P("scan", "tile", None, None, None),
        P("scan", "tile", None, None),
        P("scan", "tile"),
    )
    out_specs = (P(None, "tile", None), P(), P())
    return jax.shard_map(on_device, mesh=mesh, in_specs=in_specs, out_specs=out_specs, check_vma=False)
```

```python
import functools
import math

import jax
import jax.numpy as jnp
import numpy as np
from jax import lax
from jax.experimental import pallas as pl
from jax.experimental.pallas import tpu as pltpu
from jax.sharding import PartitionSpec as P

ITERS = 2
PS = 256
TH = 256
OW = 512
CAP = 12
NS = 8
NT = 32
SR = TH // NS
LN = 128
GRANT = 20
PAIR = 3
FLOOR2 = 0.25
REG = 1.0

OWN, NEXT, PRB, POS = 0, 2 * SR, 4 * SR, 4 * SR + 48
SEND = POS + 16
GROUP = 12

BF = jnp.bfloat16
F32 = jnp.float32


def tables():
    n = np.arange(PS, dtype=np.int64)
    angle = ((n[:, None] * n[None, :]) % PS).astype(np.float32) * np.float32(2.0 * math.pi / PS)
    c = (np.cos(angle) / np.sqrt(PS)).astype(np.float32)
    s = (np.sin(angle) / np.sqrt(PS)).astype(np.float32)
    return c, s


def table_arrays():
    return [jnp.asarray(t.astype(jnp.bfloat16)) for t in tables()]


def prepare_kernel(c_ref, s_ref, amp_ref, amp_out, m1_ref, m2_ref, sems):
    copies = [pltpu.make_async_copy(amp_ref.at[j], amp_out.at[j], sems.at[j]) for j in range(CAP)]
    for copy in copies:
        copy.start()
    c = c_ref[...]
    s = s_ref[...]
    for table, upper, lower in ((m1_ref, -s, s), (m2_ref, s, -s)):
        table[:PS, :PS] = c
        table[:PS, PS:] = upper
        table[PS:, :PS] = lower
        table[PS:, PS:] = c
    for copy in copies:
        copy.wait()


def prepare(amps):
    table = jax.ShapeDtypeStruct((2 * PS, 2 * PS), BF)
    return pl.pallas_call(
        prepare_kernel,
        out_shape=[jax.ShapeDtypeStruct(amps.shape, BF), table, table],
        in_specs=[vmem(), vmem(), pl.BlockSpec(memory_space=pltpu.HBM)],
        out_specs=[vmem()] * 3,
        scratch_shapes=[pltpu.SemaphoreType.DMA((CAP,))],
        compiler_params=params(8),
        cost_estimate=pl.CostEstimate(flops=0, bytes_accessed=8 << 20, transcendentals=0),
        name="prepare",
    )(*table_arrays(), amps)


def pattern_kernel(first, pos_ref, cnt_ref, obj_ref, halo_ref, probe_ref, amp_ref, extra_ref, m1, m2, *rest):
    if first:
        send, x, g, pg, patch, h, h2 = rest
        pr = probe_ref
    else:
        send, objn_ref, pr, x, g, pg, patch, h, h2 = rest
    count = cnt_ref[0]
    lane_blocks = [slice(q * LN, (q + 1) * LN) for q in range(4)]
    tile_start = lax.axis_index("tile") * TH
    g[...] = jnp.zeros_like(g)
    pg[...] = jnp.zeros_like(pg)
    if first:
        for q in range(4):
            x[:, q, :TH, :] = obj_ref[:, :, lane_blocks[q]]
            x[:, q, TH:, :] = halo_ref[:, :, lane_blocks[q]].astype(F32)
    else:
        for s in range(NS):
            for k in range(2):
                a = s * SR
                d = obj_ref[k, a : a + SR, :] + extra_ref[s, k * SR : (k + 1) * SR, :].astype(F32)
                e = halo_ref[k, a : a + SR, :].astype(F32) + extra_ref[s, (2 + k) * SR : (3 + k) * SR, :].astype(F32)
                objn_ref[k, a : a + SR, :] = d
                for q in range(4):
                    x[k, q, a : a + SR, :] = d[:, lane_blocks[q]]
                    x[k, q, TH + a : TH + a + SR, :] = e[:, lane_blocks[q]]
                d = extra_ref[s, 4 * SR + 16 * k : 4 * SR + 16 * (k + 1), :].astype(F32)
                for q in range(2):
                    b = a + 16 * q
                    pr[k, b : b + 16, :] = probe_ref[k, b : b + 16, :] + d[:, q * PS : (q + 1) * PS]

    def place(j):
        r = pos_ref[0, j] - tile_start
        c = pos_ref[1, j]
        base = jnp.where(c >= LN, 1, 0)
        return r, base, c - base * LN

    lanes = lax.broadcasted_iota(jnp.int32, (PS, LN), 1)

    def to_half(j, slot, live):
        r, base, off = place(j)
        head = lanes < LN - off
        turn = (LN - off) & (LN - 1)
        xs = []
        for k in range(2):
            v = [pltpu.roll(x[k, base + q, pl.ds(r, PS), :], turn, 1) for q in range(3)]
            v = jnp.concatenate([jnp.where(head, v[0], v[1]), jnp.where(head, v[1], v[2])], 1)
            patch[slot, k] = v
            xs.append(v)
        xr, xi = xs
        p0, p1 = pr[0], pr[1]
        pg[2] += (xr * xr + xi * xi) * live
        return jnp.concatenate([(p0 * xr - p1 * xi).astype(BF), (p0 * xi + p1 * xr).astype(BF)], 1)

    def half_dot(w, slot):
        for b in range(2):
            half = jnp.dot(w, m1[:, b * PS : (b + 1) * PS], preferred_element_type=F32)
            h[slot, b * PS : (b + 1) * PS, :] = half.astype(BF)

    def far_dot(slot):
        fr = jnp.dot(m2[:PS, :], h[slot], preferred_element_type=F32)
        fi = jnp.dot(m2[PS:, :], h[slot], preferred_element_type=F32)
        return fr, fi

    def update(j, live, far):
        fr, fi = far
        m = jnp.maximum(fr * fr + fi * fi, FLOOR2)
        q = amp_ref[j].astype(F32) * lax.rsqrt(m) - 1.0
        q = q * live
        return jnp.concatenate([(q * fr).astype(BF), (q * fi).astype(BF)], 1)

    def back_half_dot(u, slot):
        for b in range(2):
            half = jnp.dot(u, m2[:, b * PS : (b + 1) * PS], preferred_element_type=F32)
            h2[slot, b * PS : (b + 1) * PS, :] = half.astype(BF)

    def back_dot(slot):
        br = jnp.dot(m1[:PS, :], h2[slot], preferred_element_type=F32)
        bi = jnp.dot(m1[PS:, :], h2[slot], preferred_element_type=F32)
        return br, bi

    def add_back(j, slot, back):
        br, bi = back
        xr, xi = patch[slot, 0], patch[slot, 1]
        pg[0] += xr * br + xi * bi
        pg[1] += xr * bi - xi * br
        p0, p1 = pr[0], pr[1]
        r, base, off = place(j)
        tail = lanes >= off
        turn = off & (LN - 1)
        for k, o in enumerate((p0 * br + p1 * bi, p0 * bi - p1 * br)):
            v = [pltpu.roll(o[:, q * LN : (q + 1) * LN], turn, 1) for q in range(2)]
            g[k, base, pl.ds(r, PS), :] += jnp.where(tail, v[0], 0.0)
            g[k, base + 1, pl.ds(r, PS), :] += jnp.where(tail, v[1], v[0])
            g[k, base + 2, pl.ds(r, PS), :] += jnp.where(tail, 0.0, v[1])

    def visit(i, carry):
        j = [PAIR * i + n for n in range(PAIR)]
        live = [jnp.where(n < count, 1.0, 0.0) for n in j]
        w = to_half(j[0], 0, live[0])
        for n in range(PAIR):
            half_dot(w, n)
            if n + 1 < PAIR:
                w = to_half(j[n + 1], n + 1, live[n + 1])
        fars = [far_dot(n) for n in range(PAIR)]
        us = [update(j[n], live[n], fars[n]) for n in range(PAIR)]
        for n in range(PAIR):
            back_half_dot(us[n], n)
        backs = [back_dot(n) for n in range(PAIR)]
        for n in range(PAIR):
            add_back(j[n], n, backs[n])
        return carry

    lax.fori_loop(0, jnp.minimum((count + PAIR - 1) // PAIR, CAP // PAIR), visit, 0)
    for s in range(NS):
        a = s * SR
        for k in range(2):
            for q in range(4):
                send[s, OWN + k * SR : OWN + (k + 1) * SR, lane_blocks[q]] = g[k, q, a : a + SR, :].astype(BF)
                send[s, NEXT + k * SR : NEXT + (k + 1) * SR, lane_blocks[q]] = g[k, q, TH + a : TH + a + SR, :].astype(BF)
        for k in range(3):
            send[s, PRB + 16 * k : PRB + 16 * (k + 1), :] = jnp.concatenate(
                [pg[k, a : a + 16, :], pg[k, a + 16 : a + 32, :]], 1
            ).astype(BF)
        if first:
            send[s, POS:, :] = extra_ref[...]


def smem():
    return pl.BlockSpec(memory_space=pltpu.SMEM)


def vmem():
    return pl.BlockSpec(memory_space=pltpu.VMEM)


def params(mib):
    return pltpu.CompilerParams(vmem_limit_bytes=mib * 1024 * 1024)


def patterns(pos, cnt, obj, halo, probe, amps, tabs, posblk=None, recv=None):
    first = recv is None
    out = [jax.ShapeDtypeStruct((NS, SEND if first else POS, OW), BF)]
    if not first:
        out += [jax.ShapeDtypeStruct((2, TH, OW), F32), jax.ShapeDtypeStruct((2, PS, PS), F32)]
    args = [pos, cnt, obj, halo, probe, amps, posblk if first else recv, *tabs]
    return pl.pallas_call(
        functools.partial(pattern_kernel, first),
        out_shape=out,
        in_specs=[smem(), smem()] + [vmem()] * 7,
        out_specs=[vmem()] * len(out),
        scratch_shapes=[
            pltpu.VMEM((2, 4, 2 * TH, LN), F32),
            pltpu.VMEM((2, 4, 2 * TH, LN), F32),
            pltpu.VMEM((3, PS, PS), F32),
            pltpu.VMEM((PAIR, 2, PS, PS), F32),
            pltpu.VMEM((PAIR, 2 * PS, PS), BF),
            pltpu.VMEM((PAIR, 2 * PS, PS), BF),
        ],
        compiler_params=params(GRANT),
        name="patterns",
    )(*args)


def sum_kernel(last, recv_ref, own_ref, probe_ref, up_ref, *rest):
    def total(a, n):
        t = [recv_ref[s, a : a + n, :].astype(F32) for s in range(NS)]
        return ((t[0] + t[1]) + (t[2] + t[3])) + ((t[4] + t[5]) + (t[6] + t[7]))

    probe_ref[...] = total(PRB, 48).astype(BF)
    own_ref[...] = total(OWN, 2 * SR)
    up_ref[: 2 * SR, :] = total(NEXT, 2 * SR).astype(BF)
    if not last:
        pos = total(POS, 16)
        rest[0][...] = pos[:, :LN]
        up_ref[2 * SR :, :] = pos.astype(BF)


def sums(last, recv):
    out = [jax.ShapeDtypeStruct((2 * SR, OW), F32), jax.ShapeDtypeStruct((48, OW), BF)]
    if last:
        out += [jax.ShapeDtypeStruct((2 * SR, OW), BF)]
    else:
        out += [jax.ShapeDtypeStruct((2 * SR + 16, OW), BF), jax.ShapeDtypeStruct((16, LN), F32)]
    return pl.pallas_call(
        functools.partial(sum_kernel, last),
        out_shape=out,
        in_specs=[vmem()],
        out_specs=[vmem()] * len(out),
        compiler_params=params(8),
        name="sums",
    )(recv)


def own_kernel(pos_ref, probe_ref, own_ref, up_ref, out_ref, p2):
    for q in range(2):
        cols = slice(q * LN, (q + 1) * LN)
        p2[q, :SR, :] = jnp.zeros((SR, LN), F32)
        p2[q, SR + PS :, :] = jnp.zeros((SR, LN), F32)
        p2[q, SR : SR + PS, :] = probe_ref[0, :, cols] * probe_ref[0, :, cols] + probe_ref[1, :, cols] * probe_ref[1, :, cols]
    mine = lax.axis_index("scan") * SR
    lanes = lax.broadcasted_iota(jnp.int32, (8, LN), 1)
    parts = SR // 8

    def group(row, carry):
        shift = jnp.where(row < NS, -TH, 0) - 1

        def some(i, carry):
            carry = [list(c) for c in carry]
            for n in range(4):
                code = pos_ref[row, 4 * i + n]
                start = jnp.where(code > 0, code + shift, -4 * TH)
                c = pos_ref[row, GROUP + 4 * i + n]
                far = c >= LN
                off = jnp.where(far, c - LN, c)
                tail = lanes >= off
                turn = off & (LN - 1)
                at = jnp.clip(mine - start, -SR, PS) + SR
                for b in range(parts):
                    y0, y1 = (pltpu.roll(p2[q, pl.ds(at + 8 * b, 8), :], turn, 1) for q in range(2))
                    v = (0.0, jnp.where(tail, y0, 0.0), jnp.where(tail, y1, y0), jnp.where(tail, 0.0, y1), 0.0)
                    for q in range(4):
                        carry[b][q] = carry[b][q] + jnp.where(far, v[q], v[q + 1])
            return tuple(tuple(c) for c in carry)

        return lax.fori_loop(0, (pos_ref[row, 2 * GROUP] + 3) // 4, some, carry)

    zero = jnp.zeros((8, LN), F32)
    carry = lax.fori_loop(0, 2 * NS, group, ((zero,) * 4,) * parts)
    for q in range(4):
        cols = slice(q * LN, (q + 1) * LN)
        scale = 1.0 / (jnp.concatenate([carry[b][q] for b in range(parts)], 0) + REG)
        for k in range(2):
            a = k * SR
            out_ref[a : a + SR, cols] = ((own_ref[a : a + SR, cols] + up_ref[a : a + SR, cols].astype(F32)) * scale).astype(BF)


def own_step(pos, probe, own, up):
    return pl.pallas_call(
        own_kernel,
        out_shape=jax.ShapeDtypeStruct((2 * SR, OW), BF),
        in_specs=[smem(), vmem(), vmem(), vmem()],
        out_specs=vmem(),
        scratch_shapes=[pltpu.VMEM((2, PS + 2 * SR, LN), F32)],
        compiler_params=params(8),
        name="own_step",
    )(pos, probe, own, up)


def spread_kernel(last, *refs):
    *deltas, p0_ref, p1_ref, out_ref = refs
    probe = p0_ref[...].astype(F32) + p1_ref[...].astype(F32)
    w = probe[32:] + REG
    parts = [delta[...] for delta in deltas]
    if last:
        root = jnp.sqrt(w)
        parts += [probe[:16] / root, probe[16:32] / root, root]
    else:
        parts += [probe[:16] / w, probe[16:32] / w]
    at = 0
    for part in parts:
        n = part.shape[0]
        for s in range(NS):
            out_ref[s, at : at + n, :] = part.astype(BF)
        at += n


def spread(last, *args):
    rows = 2 * SR + 48 if last else 4 * SR + 32
    return pl.pallas_call(
        functools.partial(spread_kernel, last),
        out_shape=jax.ShapeDtypeStruct((NS, rows, OW), BF),
        in_specs=[vmem()] * len(args),
        out_specs=vmem(),
        compiler_params=params(8),
        name="spread",
    )(*args)


def final_kernel(obj_ref, probe_ref, recv_ref, obj_out, probe_out, grad_out):
    for s in range(NS):
        a = s * SR
        root = recv_ref[s, 2 * SR + 32 : 2 * SR + 48, :].astype(F32)
        for k in range(2):
            obj_out[k, a : a + SR, :] = obj_ref[k, a : a + SR, :] + recv_ref[s, k * SR : (k + 1) * SR, :].astype(F32)
            grad = recv_ref[s, 2 * SR + 16 * k : 2 * SR + 16 * (k + 1), :].astype(F32)
            d = grad / root
            for q in range(2):
                b = a + 16 * q
                grad_out[k, b : b + 16, :] = grad[:, q * PS : (q + 1) * PS]
                probe_out[k, b : b + 16, :] = probe_ref[k, b : b + 16, :] + d[:, q * PS : (q + 1) * PS]


def final(obj, probe, recv):
    return pl.pallas_call(
        final_kernel,
        out_shape=[
            jax.ShapeDtypeStruct((2, TH, OW), F32),
            jax.ShapeDtypeStruct((2, PS, PS), F32),
            jax.ShapeDtypeStruct((2, PS, PS), F32),
        ],
        in_specs=[vmem()] * 3,
        out_specs=[vmem()] * 3,
        compiler_params=params(8),
        name="final",
    )(obj, probe, recv)


def shifted(block, distance):
    return lax.ppermute(block, "tile", [(i, i + distance) for i in range(NT) if 0 <= i + distance < NT])


def swapped(block, bits):
    return lax.ppermute(block, "tile", [(i, i ^ bits) for i in range(NT)])


def four(x, swaps):
    y = [swap.astype(F32) for swap in swaps]
    return ((x.astype(F32) + y[0]) + (y[1] + y[2])).astype(BF)


def exchange(blocks):
    return lax.all_to_all(blocks, "scan", 0, 0, tiled=True)


def on_device(object_field, probe, amplitudes, positions, counts):
    pos = positions[0, 0].T
    cnt = counts[0, 0].reshape(1)
    amps, *tabs = prepare(amplitudes[0, 0])
    halo = shifted(object_field.astype(BF), -1)
    live = lax.broadcasted_iota(jnp.int32, (CAP,), 0) < cnt
    row = jnp.concatenate([jnp.where(live, pos[0] - lax.axis_index("tile") * TH + 1, 0), pos[1], cnt])
    mine = lax.broadcasted_iota(jnp.int32, (16, 1), 0) == lax.axis_index("scan")
    posblk = jnp.where(mine, row[None, :], 0).astype(BF)
    posblk = jnp.pad(posblk, ((0, 0), (0, OW - row.shape[0])))
    coded = 2 * GROUP + 1
    (send,) = patterns(pos, cnt, object_field, halo, probe, amps, tabs, posblk=posblk)
    own, part, up, tile_pos = sums(False, exchange(send))
    swaps = [swapped(part, 1), swapped(part, 2), swapped(part, 3)]
    up = shifted(up, 1)
    part = four(part, swaps)
    swaps = [swapped(part, 4), swapped(part, 8), swapped(part, 12)]
    around = jnp.concatenate([up[2 * SR :, :coded][:NS].astype(F32), tile_pos[:NS, :coded]], 0).astype(jnp.int32)
    delta = own_step(around, probe, own, up)
    part, delta = lax.optimization_barrier((four(part, swaps), delta))
    other = swapped(part, 16)
    recv = exchange(spread(False, delta, shifted(delta, -1), part, other))
    send, object_field, probe = patterns(pos, cnt, object_field, halo, probe, amps, tabs, recv=recv)
    own, part, up = sums(True, exchange(send))
    swaps = [swapped(part, 1), swapped(part, 2), swapped(part, 3)]
    up = shifted(up, 1)
    part = four(part, swaps)
    swaps = [swapped(part, 4), swapped(part, 8), swapped(part, 12)]
    delta = own_step(around, probe, own, up)
    part, delta = lax.optimization_barrier((four(part, swaps), delta))
    other = swapped(part, 16)
    recv = exchange(spread(True, delta, part, other))
    return tuple(final(object_field, probe, recv))


def solution(mesh):
    in_specs = (
        P(None, "tile", None),
        P(),
        P("scan", "tile", None, None, None),
        P("scan", "tile", None, None),
        P("scan", "tile"),
    )
    out_specs = (P(None, "tile", None), P(), P())
    return jax.shard_map(on_device, mesh=mesh, in_specs=in_specs, out_specs=out_specs, check_vma=False)
```

```python
import functools
import math

import jax
import jax.numpy as jnp
import numpy as np
from jax import lax
from jax.experimental import pallas as pl
from jax.experimental.pallas import tpu as pltpu
from jax.sharding import PartitionSpec as P

ITERS = 2
PS = 256
TH = 256
OW = 512
CAP = 12
NS = 8
NT = 32
SR = TH // NS
LN = 128
GRANT = 20
SOME = 4
UN = 8
PAIR = 3
FLOOR2 = 0.25
REG = 1.0

OWN, NEXT, PRB, POS = 0, 2 * SR, 4 * SR, 4 * SR + 48
SEND = POS + 16
GROUP = 12

BF = jnp.bfloat16
F32 = jnp.float32


def tables():
    n = np.arange(PS, dtype=np.int64)
    angle = ((n[:, None] * n[None, :]) % PS).astype(np.float32) * np.float32(2.0 * math.pi / PS)
    c = (np.cos(angle) / np.sqrt(PS)).astype(np.float32)
    s = (np.sin(angle) / np.sqrt(PS)).astype(np.float32)
    return c, s


def table_arrays():
    return [jnp.asarray(t.astype(jnp.bfloat16)) for t in tables()]


def prepare_kernel(c_ref, s_ref, amp_ref, amp_out, m1_ref, m2_ref, sems):
    copies = [pltpu.make_async_copy(amp_ref.at[j], amp_out.at[j], sems.at[j]) for j in range(CAP)]
    for copy in copies:
        copy.start()
    c = c_ref[...]
    s = s_ref[...]
    for table, upper, lower in ((m1_ref, -s, s), (m2_ref, s, -s)):
        table[:PS, :PS] = c
        table[:PS, PS:] = upper
        table[PS:, :PS] = lower
        table[PS:, PS:] = c
    for copy in copies:
        copy.wait()


def prepare(amps):
    table = jax.ShapeDtypeStruct((2 * PS, 2 * PS), BF)
    return pl.pallas_call(
        prepare_kernel,
        out_shape=[jax.ShapeDtypeStruct(amps.shape, BF), table, table],
        in_specs=[vmem(), vmem(), pl.BlockSpec(memory_space=pltpu.HBM)],
        out_specs=[vmem()] * 3,
        scratch_shapes=[pltpu.SemaphoreType.DMA((CAP,))],
        compiler_params=params(8),
        cost_estimate=pl.CostEstimate(flops=0, bytes_accessed=8 << 20, transcendentals=0),
        name="prepare",
    )(*table_arrays(), amps)


def pattern_kernel(first, pos_ref, cnt_ref, obj_ref, halo_ref, probe_ref, amp_ref, extra_ref, m1, m2, *rest):
    if first:
        send, x, g, pg, patch, h, h2 = rest
        pr = probe_ref
    else:
        send, objn_ref, pr, x, g, pg, patch, h, h2 = rest
    count = cnt_ref[0]
    lane_blocks = [slice(q * LN, (q + 1) * LN) for q in range(4)]
    tile_start = lax.axis_index("tile") * TH
    g[...] = jnp.zeros_like(g)
    pg[...] = jnp.zeros_like(pg)
    if first:
        for q in range(4):
            x[:, q, :TH, :] = obj_ref[:, :, lane_blocks[q]]
            x[:, q, TH:, :] = halo_ref[:, :, lane_blocks[q]].astype(F32)
    else:
        for s in range(NS):
            for k in range(2):
                a = s * SR
                d = obj_ref[k, a : a + SR, :] + extra_ref[s, k * SR : (k + 1) * SR, :].astype(F32)
                e = halo_ref[k, a : a + SR, :].astype(F32) + extra_ref[s, (2 + k) * SR : (3 + k) * SR, :].astype(F32)
                objn_ref[k, a : a + SR, :] = d
                for q in range(4):
                    x[k, q, a : a + SR, :] = d[:, lane_blocks[q]]
                    x[k, q, TH + a : TH + a + SR, :] = e[:, lane_blocks[q]]
                d = extra_ref[s, 4 * SR + 16 * k : 4 * SR + 16 * (k + 1), :].astype(F32)
                for q in range(2):
                    b = a + 16 * q
                    pr[k, b : b + 16, :] = probe_ref[k, b : b + 16, :] + d[:, q * PS : (q + 1) * PS]

    def place(j):
        r = pos_ref[0, j] - tile_start
        c = pos_ref[1, j]
        base = jnp.where(c >= LN, 1, 0)
        return r, base, c - base * LN

    lanes = lax.broadcasted_iota(jnp.int32, (PS, LN), 1)

    def to_half(j, slot, live):
        r, base, off = place(j)
        head = lanes < LN - off
        turn = (LN - off) & (LN - 1)
        xs = []
        for k in range(2):
            v = [pltpu.roll(x[k, base + q, pl.ds(r, PS), :], turn, 1) for q in range(3)]
            v = jnp.concatenate([jnp.where(head, v[0], v[1]), jnp.where(head, v[1], v[2])], 1)
            patch[slot, k] = v
            xs.append(v)
        xr, xi = xs
        p0, p1 = pr[0], pr[1]
        pg[2] += (xr * xr + xi * xi) * live
        return jnp.concatenate([(p0 * xr - p1 * xi).astype(BF), (p0 * xi + p1 * xr).astype(BF)], 1)

    def half_dot(w, slot):
        for b in range(2):
            half = jnp.dot(w, m1[:, b * PS : (b + 1) * PS], preferred_element_type=F32)
            h[slot, b * PS : (b + 1) * PS, :] = half.astype(BF)

    def far_dot(slot):
        fr = jnp.dot(m2[:PS, :], h[slot], preferred_element_type=F32)
        fi = jnp.dot(m2[PS:, :], h[slot], preferred_element_type=F32)
        return fr, fi

    def update(j, live, far):
        fr, fi = far
        m = jnp.maximum(fr * fr + fi * fi, FLOOR2)
        q = amp_ref[j].astype(F32) * lax.rsqrt(m) - 1.0
        q = q * live
        return jnp.concatenate([(q * fr).astype(BF), (q * fi).astype(BF)], 1)

    def back_half_dot(u, slot):
        for b in range(2):
            half = jnp.dot(u, m2[:, b * PS : (b + 1) * PS], preferred_element_type=F32)
            h2[slot, b * PS : (b + 1) * PS, :] = half.astype(BF)

    def back_dot(slot):
        br = jnp.dot(m1[:PS, :], h2[slot], preferred_element_type=F32)
        bi = jnp.dot(m1[PS:, :], h2[slot], preferred_element_type=F32)
        return br, bi

    def add_back(j, slot, back):
        br, bi = back
        xr, xi = patch[slot, 0], patch[slot, 1]
        pg[0] += xr * br + xi * bi
        pg[1] += xr * bi - xi * br
        p0, p1 = pr[0], pr[1]
        r, base, off = place(j)
        tail = lanes >= off
        turn = off & (LN - 1)
        for k, o in enumerate((p0 * br + p1 * bi, p0 * bi - p1 * br)):
            v = [pltpu.roll(o[:, q * LN : (q + 1) * LN], turn, 1) for q in range(2)]
            g[k, base, pl.ds(r, PS), :] += jnp.where(tail, v[0], 0.0)
            g[k, base + 1, pl.ds(r, PS), :] += jnp.where(tail, v[1], v[0])
            g[k, base + 2, pl.ds(r, PS), :] += jnp.where(tail, 0.0, v[1])

    def visit(i, carry):
        j = [PAIR * i + n for n in range(PAIR)]
        live = [jnp.where(n < count, 1.0, 0.0) for n in j]
        w = to_half(j[0], 0, live[0])
        for n in range(PAIR):
            half_dot(w, n)
            if n + 1 < PAIR:
                w = to_half(j[n + 1], n + 1, live[n + 1])
        fars = [far_dot(n) for n in range(PAIR)]
        us = [update(j[n], live[n], fars[n]) for n in range(PAIR)]
        for n in range(PAIR):
            back_half_dot(us[n], n)
        backs = [back_dot(n) for n in range(PAIR)]
        for n in range(PAIR):
            add_back(j[n], n, backs[n])
        return carry

    lax.fori_loop(0, jnp.minimum((count + PAIR - 1) // PAIR, CAP // PAIR), visit, 0)
    for s in range(NS):
        a = s * SR
        for k in range(2):
            for q in range(4):
                send[s, OWN + k * SR : OWN + (k + 1) * SR, lane_blocks[q]] = g[k, q, a : a + SR, :].astype(BF)
                send[s, NEXT + k * SR : NEXT + (k + 1) * SR, lane_blocks[q]] = g[k, q, TH + a : TH + a + SR, :].astype(BF)
        for k in range(3):
            send[s, PRB + 16 * k : PRB + 16 * (k + 1), :] = jnp.concatenate(
                [pg[k, a : a + 16, :], pg[k, a + 16 : a + 32, :]], 1
            ).astype(BF)
        if first:
            send[s, POS:, :] = extra_ref[...]


def smem():
    return pl.BlockSpec(memory_space=pltpu.SMEM)


def vmem():
    return pl.BlockSpec(memory_space=pltpu.VMEM)


def params(mib):
    return pltpu.CompilerParams(vmem_limit_bytes=mib * 1024 * 1024)


def patterns(pos, cnt, obj, halo, probe, amps, tabs, posblk=None, recv=None):
    first = recv is None
    out = [jax.ShapeDtypeStruct((NS, SEND if first else POS, OW), BF)]
    if not first:
        out += [jax.ShapeDtypeStruct((2, TH, OW), F32), jax.ShapeDtypeStruct((2, PS, PS), F32)]
    args = [pos, cnt, obj, halo, probe, amps, posblk if first else recv, *tabs]
    return pl.pallas_call(
        functools.partial(pattern_kernel, first),
        out_shape=out,
        in_specs=[smem(), smem()] + [vmem()] * 7,
        out_specs=[vmem()] * len(out),
        scratch_shapes=[
            pltpu.VMEM((2, 4, 2 * TH, LN), F32),
            pltpu.VMEM((2, 4, 2 * TH, LN), F32),
            pltpu.VMEM((3, PS, PS), F32),
            pltpu.VMEM((PAIR, 2, PS, PS), F32),
            pltpu.VMEM((PAIR, 2 * PS, PS), BF),
            pltpu.VMEM((PAIR, 2 * PS, PS), BF),
        ],
        compiler_params=params(GRANT),
        name="patterns",
    )(*args)


def sum_kernel(last, recv_ref, own_ref, probe_ref, up_ref, *rest):
    def total(a, n):
        t = [recv_ref[s, a : a + n, :].astype(F32) for s in range(NS)]
        return ((t[0] + t[1]) + (t[2] + t[3])) + ((t[4] + t[5]) + (t[6] + t[7]))

    probe_ref[...] = total(PRB, 48).astype(BF)
    own_ref[...] = total(OWN, 2 * SR)
    up_ref[: 2 * SR, :] = total(NEXT, 2 * SR).astype(BF)
    if not last:
        pos = total(POS, 16)
        rest[0][...] = pos[:, :LN]
        up_ref[2 * SR :, :] = pos.astype(BF)


def sums(last, recv):
    out = [jax.ShapeDtypeStruct((2 * SR, OW), F32), jax.ShapeDtypeStruct((48, OW), BF)]
    if last:
        out += [jax.ShapeDtypeStruct((2 * SR, OW), BF)]
    else:
        out += [jax.ShapeDtypeStruct((2 * SR + 16, OW), BF), jax.ShapeDtypeStruct((16, LN), F32)]
    return pl.pallas_call(
        functools.partial(sum_kernel, last),
        out_shape=out,
        in_specs=[vmem()],
        out_specs=[vmem()] * len(out),
        compiler_params=params(8),
        name="sums",
    )(recv)


def own_kernel(pos_ref, probe_ref, own_ref, up_ref, out_ref, p2, list_ref):
    for q in range(2):
        cols = slice(q * LN, (q + 1) * LN)
        p2[q, :SR, :] = jnp.zeros((SR, LN), F32)
        p2[q, SR + PS :, :] = jnp.zeros((SR, LN), F32)
        p2[q, SR : SR + PS, :] = probe_ref[0, :, cols] * probe_ref[0, :, cols] + probe_ref[1, :, cols] * probe_ref[1, :, cols]
    mine = lax.axis_index("scan") * SR + SR + 1
    lanes = lax.broadcasted_iota(jnp.int32, (8, LN), 1)
    parts = SR // 8

    def group(row, at):
        shift = mine + jnp.where(row < NS, TH, 0)

        def some(i, at):
            for n in range(SOME):
                code = pos_ref[row, SOME * i + n]
                start = shift - code
                list_ref[0, at] = start
                list_ref[1, at] = pos_ref[row, GROUP + SOME * i + n]
                at = at + jnp.where((start > 0) & (start < PS + SR) & (code > 0), 1, 0)
            return at

        return lax.fori_loop(0, (pos_ref[row, 2 * GROUP] + SOME - 1) // SOME, some, at)

    listed = lax.fori_loop(0, 2 * NS, group, 0)
    for n in range(UN):
        list_ref[0, listed + n] = 0
        list_ref[1, listed + n] = 0

    def some(i, carry):
        carry = [list(c) for c in carry]
        for n in range(UN):
            at = list_ref[0, UN * i + n]
            c = list_ref[1, UN * i + n]
            far = c >= LN
            off = jnp.where(far, c - LN, c)
            tail = lanes >= off
            turn = off & (LN - 1)
            for b in range(parts):
                y0, y1 = (pltpu.roll(p2[q, pl.ds(at + 8 * b, 8), :], turn, 1) for q in range(2))
                v = (0.0, jnp.where(tail, y0, 0.0), jnp.where(tail, y1, y0), jnp.where(tail, 0.0, y1), 0.0)
                for q in range(4):
                    carry[b][q] = carry[b][q] + jnp.where(far, v[q], v[q + 1])
        return tuple(tuple(c) for c in carry)

    zero = jnp.zeros((8, LN), F32)
    carry = lax.fori_loop(0, (listed + UN - 1) // UN, some, ((zero,) * 4,) * parts)
    for q in range(4):
        cols = slice(q * LN, (q + 1) * LN)
        scale = 1.0 / (jnp.concatenate([carry[b][q] for b in range(parts)], 0) + REG)
        for k in range(2):
            a = k * SR
            out_ref[a : a + SR, cols] = ((own_ref[a : a + SR, cols] + up_ref[a : a + SR, cols].astype(F32)) * scale).astype(BF)


def own_step(pos, probe, own, up):
    return pl.pallas_call(
        own_kernel,
        out_shape=jax.ShapeDtypeStruct((2 * SR, OW), BF),
        in_specs=[smem(), vmem(), vmem(), vmem()],
        out_specs=vmem(),
        scratch_shapes=[pltpu.VMEM((2, PS + 2 * SR, LN), F32), pltpu.SMEM((2, 2 * NS * CAP + UN), jnp.int32)],
        compiler_params=params(8),
        name="own_step",
    )(pos, probe, own, up)


def spread_kernel(last, *refs):
    *deltas, p0_ref, p1_ref, p2_ref, p3_ref, out_ref = refs
    p = [ref[...].astype(F32) for ref in (p0_ref, p1_ref, p2_ref, p3_ref)]
    probe = (p[0] + p[1]) + (p[2] + p[3])
    w = probe[32:] + REG
    parts = [delta[...] for delta in deltas]
    if last:
        root = jnp.sqrt(w)
        parts += [probe[:16] / root, probe[16:32] / root, root]
    else:
        parts += [probe[:16] / w, probe[16:32] / w]
    at = 0
    for part in parts:
        n = part.shape[0]
        for s in range(NS):
            out_ref[s, at : at + n, :] = part.astype(BF)
        at += n


def spread(last, *args):
    rows = 2 * SR + 48 if last else 4 * SR + 32
    return pl.pallas_call(
        functools.partial(spread_kernel, last),
        out_shape=jax.ShapeDtypeStruct((NS, rows, OW), BF),
        in_specs=[vmem()] * len(args),
        out_specs=vmem(),
        compiler_params=params(8),
        name="spread",
    )(*args)


def final_kernel(obj_ref, probe_ref, recv_ref, obj_out, probe_out, grad_out):
    for s in range(NS):
        a = s * SR
        root = recv_ref[s, 2 * SR + 32 : 2 * SR + 48, :].astype(F32)
        for k in range(2):
            obj_out[k, a : a + SR, :] = obj_ref[k, a : a + SR, :] + recv_ref[s, k * SR : (k + 1) * SR, :].astype(F32)
            grad = recv_ref[s, 2 * SR + 16 * k : 2 * SR + 16 * (k + 1), :].astype(F32)
            d = grad / root
            for q in range(2):
                b = a + 16 * q
                grad_out[k, b : b + 16, :] = grad[:, q * PS : (q + 1) * PS]
                probe_out[k, b : b + 16, :] = probe_ref[k, b : b + 16, :] + d[:, q * PS : (q + 1) * PS]


def final(obj, probe, recv):
    return pl.pallas_call(
        final_kernel,
        out_shape=[
            jax.ShapeDtypeStruct((2, TH, OW), F32),
            jax.ShapeDtypeStruct((2, PS, PS), F32),
            jax.ShapeDtypeStruct((2, PS, PS), F32),
        ],
        in_specs=[vmem()] * 3,
        out_specs=[vmem()] * 3,
        compiler_params=params(8),
        name="final",
    )(obj, probe, recv)


def shifted(block, distance):
    return lax.ppermute(block, "tile", [(i, (i + distance) % NT) for i in range(NT)])


def swapped(block, bits):
    return lax.ppermute(block, "tile", [(i, i ^ bits) for i in range(NT)])


def two(x, swap):
    return (x.astype(F32) + swap.astype(F32)).astype(BF)


def four(x, swaps):
    y = [swap.astype(F32) for swap in swaps]
    return ((x.astype(F32) + y[0]) + (y[1] + y[2])).astype(BF)


def exchange(blocks):
    return lax.all_to_all(blocks, "scan", 0, 0, tiled=True)


def on_device(object_field, probe, amplitudes, positions, counts):
    pos = positions[0, 0].T
    cnt = counts[0, 0].reshape(1)
    amps, *tabs = prepare(amplitudes[0, 0])
    halo = shifted(object_field.astype(BF), -1)
    live = lax.broadcasted_iota(jnp.int32, (CAP,), 0) < cnt
    row = jnp.concatenate([jnp.where(live, pos[0] - lax.axis_index("tile") * TH + 1, 0), pos[1], cnt])
    mine = lax.broadcasted_iota(jnp.int32, (16, 1), 0) == lax.axis_index("scan")
    posblk = jnp.where(mine, row[None, :], 0).astype(BF)
    posblk = jnp.pad(posblk, ((0, 0), (0, OW - row.shape[0])))
    coded = 2 * GROUP + 1
    (send,) = patterns(pos, cnt, object_field, halo, probe, amps, tabs, posblk=posblk)
    own, part, up, tile_pos = sums(False, exchange(send))
    core = swapped(part, 1)
    up = shifted(up, 1)
    part = two(part, core)
    swaps = [swapped(part, d) for d in (2, 16, 18)]
    around = jnp.concatenate([up[2 * SR :, :coded][:NS].astype(F32), tile_pos[:NS, :coded]], 0).astype(jnp.int32)
    delta = own_step(around, probe, own, up)
    part, delta = lax.optimization_barrier((four(part, swaps), delta))
    swaps = [swapped(part, d) for d in (4, 8, 12)]
    recv = exchange(spread(False, delta, shifted(delta, -1), part, *swaps))
    send, object_field, probe = patterns(pos, cnt, object_field, halo, probe, amps, tabs, recv=recv)
    own, part, up = sums(True, exchange(send))
    core = swapped(part, 1)
    up = shifted(up, 1)
    part = two(part, core)
    swaps = [swapped(part, d) for d in (2, 16, 18)]
    delta = own_step(around, probe, own, up)
    part, delta = lax.optimization_barrier((four(part, swaps), delta))
    swaps = [swapped(part, d) for d in (4, 8, 12)]
    recv = exchange(spread(True, delta, part, *swaps))
    return tuple(final(object_field, probe, recv))


def solution(mesh):
    in_specs = (
        P(None, "tile", None),
        P(),
        P("scan", "tile", None, None, None),
        P("scan", "tile", None, None),
        P("scan", "tile"),
    )
    out_specs = (P(None, "tile", None), P(), P())
    return jax.shard_map(on_device, mesh=mesh, in_specs=in_specs, out_specs=out_specs, check_vma=False)
```

```python
import functools
import math

import jax
import jax.numpy as jnp
import numpy as np
from jax import lax
from jax.experimental import pallas as pl
from jax.experimental.pallas import tpu as pltpu
from jax.sharding import PartitionSpec as P

ITERS = 2
PS = 256
TH = 256
OW = 512
CAP = 12
NS = 8
NT = 32
SR = TH // NS
LN = 128
GRANT = 20
SOME = 4
UN = 8
PAIR = 3
FLOOR2 = 0.25
REG = 1.0

OWN, NEXT, PRB, POS = 0, 2 * SR, 4 * SR, 4 * SR + 48
SEND = POS + 16
GROUP = 12

BF = jnp.bfloat16
F32 = jnp.float32


def tables():
    n = np.arange(PS, dtype=np.int64)
    angle = ((n[:, None] * n[None, :]) % PS).astype(np.float32) * np.float32(2.0 * math.pi / PS)
    c = (np.cos(angle) / np.sqrt(PS)).astype(np.float32)
    s = (np.sin(angle) / np.sqrt(PS)).astype(np.float32)
    return c, s


def prepare_kernel(c_ref, s_ref, amp_ref, m1_ref, m2_ref):
    c = c_ref[...].astype(BF)
    s = s_ref[...]
    for table, sign in ((m1_ref, -1.0), (m2_ref, 1.0)):
        table[:PS, :PS] = c
        table[:PS, PS:] = (sign * s).astype(BF)
        table[PS:, :PS] = (-sign * s).astype(BF)
        table[PS:, PS:] = c


def prepare(amps):
    table = jax.ShapeDtypeStruct((2 * PS, 2 * PS), BF)
    rounded = [jnp.asarray(t.astype(jnp.bfloat16).astype(np.float32)) for t in tables()]
    return pl.pallas_call(
        prepare_kernel,
        out_shape=[table, table],
        in_specs=[vmem()] * 3,
        out_specs=[vmem()] * 2,
        compiler_params=params(8),
        cost_estimate=pl.CostEstimate(flops=0, bytes_accessed=8 << 20, transcendentals=0),
        name="prepare",
    )(*rounded, amps)


def pattern_kernel(first, pos_ref, cnt_ref, obj_ref, halo_ref, probe_ref, amp_ref, extra_ref, m1, m2, *rest):
    if first:
        send, x, g, pg, patch, h, h2 = rest
        pr = probe_ref
    else:
        send, objn_ref, pr, x, g, pg, patch, h, h2 = rest
    count = cnt_ref[0]
    lane_blocks = [slice(q * LN, (q + 1) * LN) for q in range(4)]
    tile_start = lax.axis_index("tile") * TH
    g[...] = jnp.zeros_like(g)
    pg[...] = jnp.zeros_like(pg)
    if first:
        for q in range(4):
            x[:, q, :TH, :] = obj_ref[:, :, lane_blocks[q]]
            x[:, q, TH:, :] = halo_ref[:, :, lane_blocks[q]].astype(F32)
    else:
        for s in range(NS):
            for k in range(2):
                a = s * SR
                d = obj_ref[k, a : a + SR, :] + extra_ref[s, k * SR : (k + 1) * SR, :].astype(F32)
                e = halo_ref[k, a : a + SR, :].astype(F32) + extra_ref[s, (2 + k) * SR : (3 + k) * SR, :].astype(F32)
                objn_ref[k, a : a + SR, :] = d
                for q in range(4):
                    x[k, q, a : a + SR, :] = d[:, lane_blocks[q]]
                    x[k, q, TH + a : TH + a + SR, :] = e[:, lane_blocks[q]]
                d = extra_ref[s, 4 * SR + 16 * k : 4 * SR + 16 * (k + 1), :].astype(F32)
                for q in range(2):
                    b = a + 16 * q
                    pr[k, b : b + 16, :] = probe_ref[k, b : b + 16, :] + d[:, q * PS : (q + 1) * PS]

    def place(j):
        r = pos_ref[0, j] - tile_start
        c = pos_ref[1, j]
        base = jnp.where(c >= LN, 1, 0)
        return r, base, c - base * LN

    lanes = lax.broadcasted_iota(jnp.int32, (PS, LN), 1)

    def to_half(j, slot, live):
        r, base, off = place(j)
        head = lanes < LN - off
        turn = (LN - off) & (LN - 1)
        xs = []
        for k in range(2):
            v = [pltpu.roll(x[k, base + q, pl.ds(r, PS), :], turn, 1) for q in range(3)]
            v = jnp.concatenate([jnp.where(head, v[0], v[1]), jnp.where(head, v[1], v[2])], 1)
            patch[slot, k] = v
            xs.append(v)
        xr, xi = xs
        p0, p1 = pr[0], pr[1]
        pg[2] += (xr * xr + xi * xi) * live
        return jnp.concatenate([(p0 * xr - p1 * xi).astype(BF), (p0 * xi + p1 * xr).astype(BF)], 1)

    def half_dot(w, slot):
        for b in range(2):
            half = jnp.dot(w, m1[:, b * PS : (b + 1) * PS], preferred_element_type=F32)
            h[slot, b * PS : (b + 1) * PS, :] = half.astype(BF)

    def far_dot(slot):
        fr = jnp.dot(m2[:PS, :], h[slot], preferred_element_type=F32)
        fi = jnp.dot(m2[PS:, :], h[slot], preferred_element_type=F32)
        return fr, fi

    def update(j, live, far):
        fr, fi = far
        m = jnp.maximum(fr * fr + fi * fi, FLOOR2)
        q = amp_ref[j].astype(F32) * lax.rsqrt(m) - 1.0
        q = q * live
        return jnp.concatenate([(q * fr).astype(BF), (q * fi).astype(BF)], 1)

    def back_half_dot(u, slot):
        for b in range(2):
            half = jnp.dot(u, m2[:, b * PS : (b + 1) * PS], preferred_element_type=F32)
            h2[slot, b * PS : (b + 1) * PS, :] = half.astype(BF)

    def back_dot(slot):
        br = jnp.dot(m1[:PS, :], h2[slot], preferred_element_type=F32)
        bi = jnp.dot(m1[PS:, :], h2[slot], preferred_element_type=F32)
        return br, bi

    def add_back(j, slot, back):
        br, bi = back
        xr, xi = patch[slot, 0], patch[slot, 1]
        pg[0] += xr * br + xi * bi
        pg[1] += xr * bi - xi * br
        p0, p1 = pr[0], pr[1]
        r, base, off = place(j)
        tail = lanes >= off
        turn = off & (LN - 1)
        for k, o in enumerate((p0 * br + p1 * bi, p0 * bi - p1 * br)):
            v = [pltpu.roll(o[:, q * LN : (q + 1) * LN], turn, 1) for q in range(2)]
            g[k, base, pl.ds(r, PS), :] += jnp.where(tail, v[0], 0.0)
            g[k, base + 1, pl.ds(r, PS), :] += jnp.where(tail, v[1], v[0])
            g[k, base + 2, pl.ds(r, PS), :] += jnp.where(tail, 0.0, v[1])

    def visit(i, carry):
        j = [PAIR * i + n for n in range(PAIR)]
        live = [jnp.where(n < count, 1.0, 0.0) for n in j]
        w = to_half(j[0], 0, live[0])
        for n in range(PAIR):
            half_dot(w, n)
            if n + 1 < PAIR:
                w = to_half(j[n + 1], n + 1, live[n + 1])
        fars = [far_dot(n) for n in range(PAIR)]
        us = [update(j[n], live[n], fars[n]) for n in range(PAIR)]
        for n in range(PAIR):
            back_half_dot(us[n], n)
        backs = [back_dot(n) for n in range(PAIR)]
        for n in range(PAIR):
            add_back(j[n], n, backs[n])
        return carry

    lax.fori_loop(0, jnp.minimum((count + PAIR - 1) // PAIR, CAP // PAIR), visit, 0)
    for s in range(NS):
        a = s * SR
        for k in range(2):
            for q in range(4):
                send[s, OWN + k * SR : OWN + (k + 1) * SR, lane_blocks[q]] = g[k, q, a : a + SR, :].astype(BF)
                send[s, NEXT + k * SR : NEXT + (k + 1) * SR, lane_blocks[q]] = g[k, q, TH + a : TH + a + SR, :].astype(BF)
        for k in range(3):
            send[s, PRB + 16 * k : PRB + 16 * (k + 1), :] = jnp.concatenate(
                [pg[k, a : a + 16, :], pg[k, a + 16 : a + 32, :]], 1
            ).astype(BF)
        if first:
            send[s, POS:, :] = extra_ref[...]


def smem():
    return pl.BlockSpec(memory_space=pltpu.SMEM)


def vmem():
    return pl.BlockSpec(memory_space=pltpu.VMEM)


def params(mib):
    return pltpu.CompilerParams(vmem_limit_bytes=mib * 1024 * 1024)


def patterns(pos, cnt, obj, halo, probe, amps, tabs, posblk=None, recv=None):
    first = recv is None
    out = [jax.ShapeDtypeStruct((NS, SEND if first else POS, OW), BF)]
    if not first:
        out += [jax.ShapeDtypeStruct((2, TH, OW), F32), jax.ShapeDtypeStruct((2, PS, PS), F32)]
    args = [pos, cnt, obj, halo, probe, amps, posblk if first else recv, *tabs]
    return pl.pallas_call(
        functools.partial(pattern_kernel, first),
        out_shape=out,
        in_specs=[smem(), smem()] + [vmem()] * 7,
        out_specs=[vmem()] * len(out),
        scratch_shapes=[
            pltpu.VMEM((2, 4, 2 * TH, LN), F32),
            pltpu.VMEM((2, 4, 2 * TH, LN), F32),
            pltpu.VMEM((3, PS, PS), F32),
            pltpu.VMEM((PAIR, 2, PS, PS), F32),
            pltpu.VMEM((PAIR, 2 * PS, PS), BF),
            pltpu.VMEM((PAIR, 2 * PS, PS), BF),
        ],
        compiler_params=params(GRANT),
        name="patterns",
    )(*args)


def sum_kernel(last, recv_ref, own_ref, probe_ref, up_ref, *rest):
    def total(a, n):
        t = [recv_ref[s, a : a + n, :].astype(F32) for s in range(NS)]
        return ((t[0] + t[1]) + (t[2] + t[3])) + ((t[4] + t[5]) + (t[6] + t[7]))

    probe_ref[...] = total(PRB, 48).astype(BF)
    own_ref[...] = total(OWN, 2 * SR)
    up_ref[: 2 * SR, :] = total(NEXT, 2 * SR).astype(BF)
    if not last:
        pos = total(POS, 16)
        rest[0][...] = pos[:, :LN]
        up_ref[2 * SR :, :] = pos.astype(BF)


def sums(last, recv):
    out = [jax.ShapeDtypeStruct((2 * SR, OW), F32), jax.ShapeDtypeStruct((48, OW), BF)]
    if last:
        out += [jax.ShapeDtypeStruct((2 * SR, OW), BF)]
    else:
        out += [jax.ShapeDtypeStruct((2 * SR + 16, OW), BF), jax.ShapeDtypeStruct((16, LN), F32)]
    return pl.pallas_call(
        functools.partial(sum_kernel, last),
        out_shape=out,
        in_specs=[vmem()],
        out_specs=[vmem()] * len(out),
        compiler_params=params(8),
        name="sums",
    )(recv)


def own_kernel(pos_ref, probe_ref, own_ref, up_ref, out_ref, p2, list_ref):
    for q in range(2):
        cols = slice(q * LN, (q + 1) * LN)
        p2[q, :SR, :] = jnp.zeros((SR, LN), F32)
        p2[q, SR + PS :, :] = jnp.zeros((SR, LN), F32)
        p2[q, SR : SR + PS, :] = probe_ref[0, :, cols] * probe_ref[0, :, cols] + probe_ref[1, :, cols] * probe_ref[1, :, cols]
    mine = lax.axis_index("scan") * SR + SR + 1
    lanes = lax.broadcasted_iota(jnp.int32, (8, LN), 1)
    parts = SR // 8

    def group(row, at):
        shift = mine + jnp.where(row < NS, TH, 0)

        def some(i, at):
            for n in range(SOME):
                code = pos_ref[row, SOME * i + n]
                start = shift - code
                list_ref[0, at] = start
                list_ref[1, at] = pos_ref[row, GROUP + SOME * i + n]
                at = at + jnp.where((start > 0) & (start < PS + SR) & (code > 0), 1, 0)
            return at

        return lax.fori_loop(0, (pos_ref[row, 2 * GROUP] + SOME - 1) // SOME, some, at)

    listed = lax.fori_loop(0, 2 * NS, group, 0)
    for n in range(UN):
        list_ref[0, listed + n] = 0
        list_ref[1, listed + n] = 0

    def some(i, carry):
        carry = [list(c) for c in carry]
        for n in range(UN):
            at = list_ref[0, UN * i + n]
            c = list_ref[1, UN * i + n]
            far = c >= LN
            off = jnp.where(far, c - LN, c)
            tail = lanes >= off
            turn = off & (LN - 1)
            for b in range(parts):
                y0, y1 = (pltpu.roll(p2[q, pl.ds(at + 8 * b, 8), :], turn, 1) for q in range(2))
                v = (0.0, jnp.where(tail, y0, 0.0), jnp.where(tail, y1, y0), jnp.where(tail, 0.0, y1), 0.0)
                for q in range(4):
                    carry[b][q] = carry[b][q] + jnp.where(far, v[q], v[q + 1])
        return tuple(tuple(c) for c in carry)

    zero = jnp.zeros((8, LN), F32)
    carry = lax.fori_loop(0, (listed + UN - 1) // UN, some, ((zero,) * 4,) * parts)
    for q in range(4):
        cols = slice(q * LN, (q + 1) * LN)
        scale = 1.0 / (jnp.concatenate([carry[b][q] for b in range(parts)], 0) + REG)
        for k in range(2):
            a = k * SR
            out_ref[a : a + SR, cols] = ((own_ref[a : a + SR, cols] + up_ref[a : a + SR, cols].astype(F32)) * scale).astype(BF)


def own_step(pos, probe, own, up):
    return pl.pallas_call(
        own_kernel,
        out_shape=jax.ShapeDtypeStruct((2 * SR, OW), BF),
        in_specs=[smem(), vmem(), vmem(), vmem()],
        out_specs=vmem(),
        scratch_shapes=[pltpu.VMEM((2, PS + 2 * SR, LN), F32), pltpu.SMEM((2, 2 * NS * CAP + UN), jnp.int32)],
        compiler_params=params(8),
        name="own_step",
    )(pos, probe, own, up)


def spread_kernel(last, *refs):
    *deltas, p0_ref, p1_ref, p2_ref, p3_ref, out_ref = refs
    p = [ref[...].astype(F32) for ref in (p0_ref, p1_ref, p2_ref, p3_ref)]
    probe = (p[0] + p[1]) + (p[2] + p[3])
    w = probe[32:] + REG
    parts = [delta[...] for delta in deltas]
    if last:
        root = jnp.sqrt(w)
        parts += [probe[:16] / root, probe[16:32] / root, root]
    else:
        parts += [probe[:16] / w, probe[16:32] / w]
    at = 0
    for part in parts:
        n = part.shape[0]
        for s in range(NS):
            out_ref[s, at : at + n, :] = part.astype(BF)
        at += n


def spread(last, *args):
    rows = 2 * SR + 48 if last else 4 * SR + 32
    return pl.pallas_call(
        functools.partial(spread_kernel, last),
        out_shape=jax.ShapeDtypeStruct((NS, rows, OW), BF),
        in_specs=[vmem()] * len(args),
        out_specs=vmem(),
        compiler_params=params(8),
        name="spread",
    )(*args)


def final_kernel(obj_ref, probe_ref, recv_ref, obj_out, probe_out, grad_out):
    for s in range(NS):
        a = s * SR
        root = recv_ref[s, 2 * SR + 32 : 2 * SR + 48, :].astype(F32)
        for k in range(2):
            obj_out[k, a : a + SR, :] = obj_ref[k, a : a + SR, :] + recv_ref[s, k * SR : (k + 1) * SR, :].astype(F32)
            grad = recv_ref[s, 2 * SR + 16 * k : 2 * SR + 16 * (k + 1), :].astype(F32)
            d = grad / root
            for q in range(2):
                b = a + 16 * q
                grad_out[k, b : b + 16, :] = grad[:, q * PS : (q + 1) * PS]
                probe_out[k, b : b + 16, :] = probe_ref[k, b : b + 16, :] + d[:, q * PS : (q + 1) * PS]


def final(obj, probe, recv):
    return pl.pallas_call(
        final_kernel,
        out_shape=[
            jax.ShapeDtypeStruct((2, TH, OW), F32),
            jax.ShapeDtypeStruct((2, PS, PS), F32),
            jax.ShapeDtypeStruct((2, PS, PS), F32),
        ],
        in_specs=[vmem()] * 3,
        out_specs=[vmem()] * 3,
        compiler_params=params(8),
        name="final",
    )(obj, probe, recv)


def shifted(block, distance):
    return lax.ppermute(block, "tile", [(i, (i + distance) % NT) for i in range(NT)])


def swapped(block, bits):
    return lax.ppermute(block, "tile", [(i, i ^ bits) for i in range(NT)])


def two(x, swap):
    return (x.astype(F32) + swap.astype(F32)).astype(BF)


def four(x, swaps):
    y = [swap.astype(F32) for swap in swaps]
    return ((x.astype(F32) + y[0]) + (y[1] + y[2])).astype(BF)


def exchange(blocks):
    return lax.all_to_all(blocks, "scan", 0, 0, tiled=True)


def on_device(object_field, probe, amplitudes, positions, counts):
    pos = positions[0, 0].T
    cnt = counts[0, 0].reshape(1)
    amps = amplitudes[0, 0]
    tabs = prepare(amps)
    halo = shifted(object_field.astype(BF), -1)
    live = lax.broadcasted_iota(jnp.int32, (CAP,), 0) < cnt
    row = jnp.concatenate([jnp.where(live, pos[0] - lax.axis_index("tile") * TH + 1, 0), pos[1], cnt])
    mine = lax.broadcasted_iota(jnp.int32, (16, 1), 0) == lax.axis_index("scan")
    posblk = jnp.where(mine, row[None, :], 0).astype(BF)
    posblk = jnp.pad(posblk, ((0, 0), (0, OW - row.shape[0])))
    coded = 2 * GROUP + 1
    (send,) = patterns(pos, cnt, object_field, halo, probe, amps, tabs, posblk=posblk)
    own, part, up, tile_pos = sums(False, exchange(send))
    core = swapped(part, 1)
    up = shifted(up, 1)
    part = two(part, core)
    swaps = [swapped(part, d) for d in (2, 16, 18)]
    around = jnp.concatenate([up[2 * SR :, :coded][:NS].astype(F32), tile_pos[:NS, :coded]], 0).astype(jnp.int32)
    delta = own_step(around, probe, own, up)
    part, delta = lax.optimization_barrier((four(part, swaps), delta))
    swaps = [swapped(part, d) for d in (4, 8, 12)]
    recv = exchange(spread(False, delta, shifted(delta, -1), part, *swaps))
    send, object_field, probe = patterns(pos, cnt, object_field, halo, probe, amps, tabs, recv=recv)
    own, part, up = sums(True, exchange(send))
    core = swapped(part, 1)
    up = shifted(up, 1)
    part = two(part, core)
    swaps = [swapped(part, d) for d in (2, 16, 18)]
    delta = own_step(around, probe, own, up)
    part = four(part, swaps)
    swaps = [swapped(part, d) for d in (4, 8, 12)]
    recv = exchange(spread(True, delta, part, *swaps))
    return tuple(final(object_field, probe, recv))


def solution(mesh):
    in_specs = (
        P(None, "tile", None),
        P(),
        P("scan", "tile", None, None, None),
        P("scan", "tile", None, None),
        P("scan", "tile"),
    )
    out_specs = (P(None, "tile", None), P(), P())
    return jax.shard_map(on_device, mesh=mesh, in_specs=in_specs, out_specs=out_specs, check_vma=False)
```

```python
import functools
import math

import jax
import jax.numpy as jnp
import numpy as np
from jax import lax
from jax.experimental import pallas as pl
from jax.experimental.pallas import tpu as pltpu
from jax.sharding import PartitionSpec as P

ITERS = 2
PS = 256
TH = 256
OW = 512
CAP = 12
NS = 8
NT = 32
SR = TH // NS
LN = 128
GRANT = 20
SOME = 4
UN = 8
PAIR = 3
FLOOR2 = 0.25
REG = 1.0

OWN, NEXT, PRB, POS = 0, 2 * SR, 4 * SR, 4 * SR + 48
SEND = POS + 16
GROUP = 12

BF = jnp.bfloat16
F32 = jnp.float32


def tables():
    n = np.arange(PS, dtype=np.int64)
    angle = ((n[:, None] * n[None, :]) % PS).astype(np.float32) * np.float32(2.0 * math.pi / PS)
    c = (np.cos(angle) / np.sqrt(PS)).astype(np.float32)
    s = (np.sin(angle) / np.sqrt(PS)).astype(np.float32)
    return c, s


def prepare_kernel(tab_ref, amp_ref, amp_out, m1_ref, m2_ref):
    amp_out[...] = amp_ref[...]
    c = tab_ref[0].astype(BF)
    s = tab_ref[1]
    for table, sign in ((m1_ref, -1.0), (m2_ref, 1.0)):
        table[:PS, :PS] = c
        table[:PS, PS:] = (sign * s).astype(BF)
        table[PS:, :PS] = (-sign * s).astype(BF)
        table[PS:, PS:] = c


def prepare(amps):
    table = jax.ShapeDtypeStruct((2 * PS, 2 * PS), BF)
    rounded = jnp.asarray(np.stack(tables()).astype(jnp.bfloat16).astype(np.float32))
    return pl.pallas_call(
        prepare_kernel,
        out_shape=[jax.ShapeDtypeStruct(amps.shape, BF), table, table],
        in_specs=[vmem()] * 2,
        out_specs=[vmem()] * 3,
        compiler_params=params(8),
        cost_estimate=pl.CostEstimate(flops=0, bytes_accessed=8 << 20, transcendentals=0),
        name="prepare",
    )(rounded, amps)


def pattern_kernel(first, pos_ref, cnt_ref, obj_ref, halo_ref, probe_ref, amp_ref, extra_ref, m1, m2, *rest):
    if first:
        send, x, g, pg, patch, h, h2 = rest
        pr = probe_ref
    else:
        send, objn_ref, pr, x, g, pg, patch, h, h2 = rest
    count = cnt_ref[0]
    lane_blocks = [slice(q * LN, (q + 1) * LN) for q in range(4)]
    tile_start = lax.axis_index("tile") * TH
    g[...] = jnp.zeros_like(g)
    pg[...] = jnp.zeros_like(pg)
    if first:
        for q in range(4):
            x[:, q, :TH, :] = obj_ref[:, :, lane_blocks[q]]
            x[:, q, TH:, :] = halo_ref[:, :, lane_blocks[q]].astype(F32)
    else:
        for s in range(NS):
            for k in range(2):
                a = s * SR
                d = obj_ref[k, a : a + SR, :] + extra_ref[s, k * SR : (k + 1) * SR, :].astype(F32)
                e = halo_ref[k, a : a + SR, :].astype(F32) + extra_ref[s, (2 + k) * SR : (3 + k) * SR, :].astype(F32)
                objn_ref[k, a : a + SR, :] = d
                for q in range(4):
                    x[k, q, a : a + SR, :] = d[:, lane_blocks[q]]
                    x[k, q, TH + a : TH + a + SR, :] = e[:, lane_blocks[q]]
                d = extra_ref[s, 4 * SR + 16 * k : 4 * SR + 16 * (k + 1), :].astype(F32)
                for q in range(2):
                    b = a + 16 * q
                    pr[k, b : b + 16, :] = probe_ref[k, b : b + 16, :] + d[:, q * PS : (q + 1) * PS]

    def place(j):
        r = pos_ref[0, j] - tile_start
        c = pos_ref[1, j]
        base = jnp.where(c >= LN, 1, 0)
        return r, base, c - base * LN

    lanes = lax.broadcasted_iota(jnp.int32, (PS, LN), 1)

    def to_half(j, slot, live):
        r, base, off = place(j)
        head = lanes < LN - off
        turn = (LN - off) & (LN - 1)
        xs = []
        for k in range(2):
            v = [pltpu.roll(x[k, base + q, pl.ds(r, PS), :], turn, 1) for q in range(3)]
            v = jnp.concatenate([jnp.where(head, v[0], v[1]), jnp.where(head, v[1], v[2])], 1)
            patch[slot, k] = v
            xs.append(v)
        xr, xi = xs
        p0, p1 = pr[0], pr[1]
        pg[2] += (xr * xr + xi * xi) * live
        return jnp.concatenate([(p0 * xr - p1 * xi).astype(BF), (p0 * xi + p1 * xr).astype(BF)], 1)

    def half_dot(w, slot):
        for b in range(2):
            half = jnp.dot(w, m1[:, b * PS : (b + 1) * PS], preferred_element_type=F32)
            h[slot, b * PS : (b + 1) * PS, :] = half.astype(BF)

    def far_dot(slot):
        fr = jnp.dot(m2[:PS, :], h[slot], preferred_element_type=F32)
        fi = jnp.dot(m2[PS:, :], h[slot], preferred_element_type=F32)
        return fr, fi

    def update(j, live, far):
        fr, fi = far
        m = jnp.maximum(fr * fr + fi * fi, FLOOR2)
        q = amp_ref[j].astype(F32) * lax.rsqrt(m) - 1.0
        q = q * live
        return jnp.concatenate([(q * fr).astype(BF), (q * fi).astype(BF)], 1)

    def back_half_dot(u, slot):
        for b in range(2):
            half = jnp.dot(u, m2[:, b * PS : (b + 1) * PS], preferred_element_type=F32)
            h2[slot, b * PS : (b + 1) * PS, :] = half.astype(BF)

    def back_dot(slot):
        br = jnp.dot(m1[:PS, :], h2[slot], preferred_element_type=F32)
        bi = jnp.dot(m1[PS:, :], h2[slot], preferred_element_type=F32)
        return br, bi

    def add_back(j, slot, back):
        br, bi = back
        xr, xi = patch[slot, 0], patch[slot, 1]
        pg[0] += xr * br + xi * bi
        pg[1] += xr * bi - xi * br
        p0, p1 = pr[0], pr[1]
        r, base, off = place(j)
        tail = lanes >= off
        turn = off & (LN - 1)
        for k, o in enumerate((p0 * br + p1 * bi, p0 * bi - p1 * br)):
            v = [pltpu.roll(o[:, q * LN : (q + 1) * LN], turn, 1) for q in range(2)]
            g[k, base, pl.ds(r, PS), :] += jnp.where(tail, v[0], 0.0)
            g[k, base + 1, pl.ds(r, PS), :] += jnp.where(tail, v[1], v[0])
            g[k, base + 2, pl.ds(r, PS), :] += jnp.where(tail, 0.0, v[1])

    def visit(i, carry):
        j = [PAIR * i + n for n in range(PAIR)]
        live = [jnp.where(n < count, 1.0, 0.0) for n in j]
        w = to_half(j[0], 0, live[0])
        for n in range(PAIR):
            half_dot(w, n)
            if n + 1 < PAIR:
                w = to_half(j[n + 1], n + 1, live[n + 1])
        fars = [far_dot(n) for n in range(PAIR)]
        us = [update(j[n], live[n], fars[n]) for n in range(PAIR)]
        for n in range(PAIR):
            back_half_dot(us[n], n)
        backs = [back_dot(n) for n in range(PAIR)]
        for n in range(PAIR):
            add_back(j[n], n, backs[n])
        return carry

    lax.fori_loop(0, jnp.minimum((count + PAIR - 1) // PAIR, CAP // PAIR), visit, 0)
    for s in range(NS):
        a = s * SR
        for k in range(2):
            for q in range(4):
                send[s, OWN + k * SR : OWN + (k + 1) * SR, lane_blocks[q]] = g[k, q, a : a + SR, :].astype(BF)
                send[s, NEXT + k * SR : NEXT + (k + 1) * SR, lane_blocks[q]] = g[k, q, TH + a : TH + a + SR, :].astype(BF)
        for k in range(3):
            send[s, PRB + 16 * k : PRB + 16 * (k + 1), :] = jnp.concatenate(
                [pg[k, a : a + 16, :], pg[k, a + 16 : a + 32, :]], 1
            ).astype(BF)
        if first:
            send[s, POS:, :] = extra_ref[...]


def smem():
    return pl.BlockSpec(memory_space=pltpu.SMEM)


def vmem():
    return pl.BlockSpec(memory_space=pltpu.VMEM)


def params(mib):
    return pltpu.CompilerParams(vmem_limit_bytes=mib * 1024 * 1024)


def patterns(pos, cnt, obj, halo, probe, amps, tabs, posblk=None, recv=None):
    first = recv is None
    out = [jax.ShapeDtypeStruct((NS, SEND if first else POS, OW), BF)]
    if not first:
        out += [jax.ShapeDtypeStruct((2, TH, OW), F32), jax.ShapeDtypeStruct((2, PS, PS), F32)]
    args = [pos, cnt, obj, halo, probe, amps, posblk if first else recv, *tabs]
    return pl.pallas_call(
        functools.partial(pattern_kernel, first),
        out_shape=out,
        in_specs=[smem(), smem()] + [vmem()] * 7,
        out_specs=[vmem()] * len(out),
        scratch_shapes=[
            pltpu.VMEM((2, 4, 2 * TH, LN), F32),
            pltpu.VMEM((2, 4, 2 * TH, LN), F32),
            pltpu.VMEM((3, PS, PS), F32),
            pltpu.VMEM((PAIR, 2, PS, PS), F32),
            pltpu.VMEM((PAIR, 2 * PS, PS), BF),
            pltpu.VMEM((PAIR, 2 * PS, PS), BF),
        ],
        compiler_params=params(GRANT),
        name="patterns",
    )(*args)


def sum_kernel(last, recv_ref, own_ref, probe_ref, up_ref, *rest):
    def total(a, n):
        t = [recv_ref[s, a : a + n, :].astype(F32) for s in range(NS)]
        return ((t[0] + t[1]) + (t[2] + t[3])) + ((t[4] + t[5]) + (t[6] + t[7]))

    probe_ref[...] = total(PRB, 48).astype(BF)
    own_ref[...] = total(OWN, 2 * SR)
    up_ref[: 2 * SR, :] = total(NEXT, 2 * SR).astype(BF)
    if not last:
        pos = total(POS, 16)
        rest[0][...] = pos[:, :LN]
        up_ref[2 * SR :, :] = pos.astype(BF)


def sums(last, recv):
    out = [jax.ShapeDtypeStruct((2 * SR, OW), F32), jax.ShapeDtypeStruct((48, OW), BF)]
    if last:
        out += [jax.ShapeDtypeStruct((2 * SR, OW), BF)]
    else:
        out += [jax.ShapeDtypeStruct((2 * SR + 16, OW), BF), jax.ShapeDtypeStruct((16, LN), F32)]
    return pl.pallas_call(
        functools.partial(sum_kernel, last),
        out_shape=out,
        in_specs=[vmem()],
        out_specs=[vmem()] * len(out),
        compiler_params=params(8),
        name="sums",
    )(recv)


def own_kernel(pos_ref, probe_ref, own_ref, up_ref, out_ref, p2, list_ref):
    for q in range(2):
        cols = slice(q * LN, (q + 1) * LN)
        p2[q, :SR, :] = jnp.zeros((SR, LN), F32)
        p2[q, SR + PS :, :] = jnp.zeros((SR, LN), F32)
        p2[q, SR : SR + PS, :] = probe_ref[0, :, cols] * probe_ref[0, :, cols] + probe_ref[1, :, cols] * probe_ref[1, :, cols]
    mine = lax.axis_index("scan") * SR + SR + 1
    lanes = lax.broadcasted_iota(jnp.int32, (8, LN), 1)
    parts = SR // 8

    def group(row, at):
        shift = mine + jnp.where(row < NS, TH, 0)

        def some(i, at):
            for n in range(SOME):
                code = pos_ref[row, SOME * i + n]
                start = shift - code
                list_ref[0, at] = start
                list_ref[1, at] = pos_ref[row, GROUP + SOME * i + n]
                at = at + jnp.where((start > 0) & (start < PS + SR) & (code > 0), 1, 0)
            return at

        return lax.fori_loop(0, (pos_ref[row, 2 * GROUP] + SOME - 1) // SOME, some, at)

    listed = lax.fori_loop(0, 2 * NS, group, 0)
    for n in range(UN):
        list_ref[0, listed + n] = 0
        list_ref[1, listed + n] = 0

    def some(i, carry):
        carry = [list(c) for c in carry]
        for n in range(UN):
            at = list_ref[0, UN * i + n]
            c = list_ref[1, UN * i + n]
            far = c >= LN
            off = jnp.where(far, c - LN, c)
            tail = lanes >= off
            turn = off & (LN - 1)
            for b in range(parts):
                y0, y1 = (pltpu.roll(p2[q, pl.ds(at + 8 * b, 8), :], turn, 1) for q in range(2))
                v = (0.0, jnp.where(tail, y0, 0.0), jnp.where(tail, y1, y0), jnp.where(tail, 0.0, y1), 0.0)
                for q in range(4):
                    carry[b][q] = carry[b][q] + jnp.where(far, v[q], v[q + 1])
        return tuple(tuple(c) for c in carry)

    zero = jnp.zeros((8, LN), F32)
    carry = lax.fori_loop(0, (listed + UN - 1) // UN, some, ((zero,) * 4,) * parts)
    for q in range(4):
        cols = slice(q * LN, (q + 1) * LN)
        scale = 1.0 / (jnp.concatenate([carry[b][q] for b in range(parts)], 0) + REG)
        for k in range(2):
            a = k * SR
            out_ref[a : a + SR, cols] = ((own_ref[a : a + SR, cols] + up_ref[a : a + SR, cols].astype(F32)) * scale).astype(BF)


def own_step(pos, probe, own, up):
    return pl.pallas_call(
        own_kernel,
        out_shape=jax.ShapeDtypeStruct((2 * SR, OW), BF),
        in_specs=[smem(), vmem(), vmem(), vmem()],
        out_specs=vmem(),
        scratch_shapes=[pltpu.VMEM((2, PS + 2 * SR, LN), F32), pltpu.SMEM((2, 2 * NS * CAP + UN), jnp.int32)],
        compiler_params=params(8),
        name="own_step",
    )(pos, probe, own, up)


def spread_kernel(last, *refs):
    *deltas, p0_ref, p1_ref, p2_ref, p3_ref, out_ref = refs
    p = [ref[...].astype(F32) for ref in (p0_ref, p1_ref, p2_ref, p3_ref)]
    probe = (p[0] + p[1]) + (p[2] + p[3])
    w = probe[32:] + REG
    parts = [delta[...] for delta in deltas]
    if last:
        root = jnp.sqrt(w)
        parts += [probe[:16] / root, probe[16:32] / root, root]
    else:
        parts += [probe[:16] / w, probe[16:32] / w]
    at = 0
    for part in parts:
        n = part.shape[0]
        for s in range(NS):
            out_ref[s, at : at + n, :] = part.astype(BF)
        at += n


def spread(last, *args):
    rows = 2 * SR + 48 if last else 4 * SR + 32
    return pl.pallas_call(
        functools.partial(spread_kernel, last),
        out_shape=jax.ShapeDtypeStruct((NS, rows, OW), BF),
        in_specs=[vmem()] * len(args),
        out_specs=vmem(),
        compiler_params=params(8),
        name="spread",
    )(*args)


def final_kernel(obj_ref, probe_ref, recv_ref, obj_out, probe_out, grad_out):
    for s in range(NS):
        a = s * SR
        root = recv_ref[s, 2 * SR + 32 : 2 * SR + 48, :].astype(F32)
        for k in range(2):
            obj_out[k, a : a + SR, :] = obj_ref[k, a : a + SR, :] + recv_ref[s, k * SR : (k + 1) * SR, :].astype(F32)
            grad = recv_ref[s, 2 * SR + 16 * k : 2 * SR + 16 * (k + 1), :].astype(F32)
            d = grad / root
            for q in range(2):
                b = a + 16 * q
                grad_out[k, b : b + 16, :] = grad[:, q * PS : (q + 1) * PS]
                probe_out[k, b : b + 16, :] = probe_ref[k, b : b + 16, :] + d[:, q * PS : (q + 1) * PS]


def final(obj, probe, recv):
    return pl.pallas_call(
        final_kernel,
        out_shape=[
            jax.ShapeDtypeStruct((2, TH, OW), F32),
            jax.ShapeDtypeStruct((2, PS, PS), F32),
            jax.ShapeDtypeStruct((2, PS, PS), F32),
        ],
        in_specs=[vmem()] * 3,
        out_specs=[vmem()] * 3,
        compiler_params=params(8),
        name="final",
    )(obj, probe, recv)


def shifted(block, distance):
    return lax.ppermute(block, "tile", [(i, (i + distance) % NT) for i in range(NT)])


def swapped(block, bits):
    return lax.ppermute(block, "tile", [(i, i ^ bits) for i in range(NT)])


def two(x, swap):
    return (x.astype(F32) + swap.astype(F32)).astype(BF)


def four(x, swaps):
    y = [swap.astype(F32) for swap in swaps]
    return ((x.astype(F32) + y[0]) + (y[1] + y[2])).astype(BF)


def exchange(blocks):
    return lax.all_to_all(blocks, "scan", 0, 0, tiled=True)


def on_device(object_field, probe, amplitudes, positions, counts):
    pos = positions[0, 0].T
    cnt = counts[0, 0].reshape(1)
    amps, *tabs = prepare(amplitudes[0, 0])
    halo = shifted(object_field.astype(BF), -1)
    live = lax.broadcasted_iota(jnp.int32, (CAP,), 0) < cnt
    row = jnp.concatenate([jnp.where(live, pos[0] - lax.axis_index("tile") * TH + 1, 0), pos[1], cnt])
    mine = lax.broadcasted_iota(jnp.int32, (16, 1), 0) == lax.axis_index("scan")
    posblk = jnp.where(mine, row[None, :], 0).astype(BF)
    posblk = jnp.pad(posblk, ((0, 0), (0, OW - row.shape[0])))
    coded = 2 * GROUP + 1
    (send,) = patterns(pos, cnt, object_field, halo, probe, amps, tabs, posblk=posblk)
    own, part, up, tile_pos = sums(False, exchange(send))
    core = swapped(part, 1)
    up = shifted(up, 1)
    part = two(part, core)
    swaps = [swapped(part, d) for d in (2, 16, 18)]
    around = jnp.concatenate([up[2 * SR :, :coded][:NS].astype(F32), tile_pos[:NS, :coded]], 0).astype(jnp.int32)
    delta = own_step(around, probe, own, up)
    part, delta = lax.optimization_barrier((four(part, swaps), delta))
    swaps = [swapped(part, d) for d in (4, 8, 12)]
    recv = exchange(spread(False, delta, shifted(delta, -1), part, *swaps))
    send, object_field, probe = patterns(pos, cnt, object_field, halo, probe, amps, tabs, recv=recv)
    own, part, up = sums(True, exchange(send))
    core = swapped(part, 1)
    up = shifted(up, 1)
    part = two(part, core)
    swaps = [swapped(part, d) for d in (2, 16, 18)]
    delta = own_step(around, probe, own, up)
    part = four(part, swaps)
    swaps = [swapped(part, d) for d in (4, 8, 12)]
    recv = exchange(spread(True, delta, part, *swaps))
    return tuple(final(object_field, probe, recv))


def solution(mesh):
    in_specs = (
        P(None, "tile", None),
        P(),
        P("scan", "tile", None, None, None),
        P("scan", "tile", None, None),
        P("scan", "tile"),
    )
    out_specs = (P(None, "tile", None), P(), P())
    return jax.shard_map(on_device, mesh=mesh, in_specs=in_specs, out_specs=out_specs, check_vma=False)
```

```python
import functools
import math

import jax
import jax.numpy as jnp
import numpy as np
from jax import lax
from jax.experimental import pallas as pl
from jax.experimental.pallas import tpu as pltpu
from jax.sharding import PartitionSpec as P

ITERS = 2
PS = 256
TH = 256
OW = 512
CAP = 12
NS = 8
NT = 32
SR = TH // NS
LN = 128
GRANT = 20
SOME = 4
UN = 8
PAIR = 4
FLOOR2 = 0.25
REG = 1.0

OWN, NEXT, PRB, POS = 0, 2 * SR, 4 * SR, 4 * SR + 48
SEND = POS + 16
GROUP = 12

BF = jnp.bfloat16
F32 = jnp.float32


def tables():
    n = np.arange(PS, dtype=np.int64)
    angle = ((n[:, None] * n[None, :]) % PS).astype(np.float32) * np.float32(2.0 * math.pi / PS)
    c = (np.cos(angle) / np.sqrt(PS)).astype(np.float32)
    s = (np.sin(angle) / np.sqrt(PS)).astype(np.float32)
    return c, s


def prepare_kernel(tab_ref, amp_ref, amp_out, m1_ref, m2_ref):
    amp_out[...] = amp_ref[...]
    c = tab_ref[0].astype(BF)
    s = tab_ref[1]
    for table, sign in ((m1_ref, -1.0), (m2_ref, 1.0)):
        table[:PS, :PS] = c
        table[:PS, PS:] = (sign * s).astype(BF)
        table[PS:, :PS] = (-sign * s).astype(BF)
        table[PS:, PS:] = c


def prepare(amps):
    table = jax.ShapeDtypeStruct((2 * PS, 2 * PS), BF)
    rounded = jnp.asarray(np.stack(tables()).astype(jnp.bfloat16).astype(np.float32))
    return pl.pallas_call(
        prepare_kernel,
        out_shape=[jax.ShapeDtypeStruct(amps.shape, BF), table, table],
        in_specs=[vmem()] * 2,
        out_specs=[vmem()] * 3,
        compiler_params=params(8),
        cost_estimate=pl.CostEstimate(flops=0, bytes_accessed=8 << 20, transcendentals=0),
        name="prepare",
    )(rounded, amps)


def pattern_kernel(first, pos_ref, cnt_ref, obj_ref, halo_ref, probe_ref, amp_ref, extra_ref, m1, m2, *rest):
    if first:
        send, x, g, pg, patch, h, h2 = rest
        pr = probe_ref
    else:
        send, objn_ref, pr, x, g, pg, patch, h, h2 = rest
    count = cnt_ref[0]
    lane_blocks = [slice(q * LN, (q + 1) * LN) for q in range(4)]
    tile_start = lax.axis_index("tile") * TH
    g[...] = jnp.zeros_like(g)
    pg[...] = jnp.zeros_like(pg)
    if first:
        for q in range(4):
            x[:, q, :TH, :] = obj_ref[:, :, lane_blocks[q]]
            x[:, q, TH:, :] = halo_ref[:, :, lane_blocks[q]].astype(F32)
    else:
        for s in range(NS):
            for k in range(2):
                a = s * SR
                d = obj_ref[k, a : a + SR, :] + extra_ref[s, k * SR : (k + 1) * SR, :].astype(F32)
                e = halo_ref[k, a : a + SR, :].astype(F32) + extra_ref[s, (2 + k) * SR : (3 + k) * SR, :].astype(F32)
                objn_ref[k, a : a + SR, :] = d
                for q in range(4):
                    x[k, q, a : a + SR, :] = d[:, lane_blocks[q]]
                    x[k, q, TH + a : TH + a + SR, :] = e[:, lane_blocks[q]]
                d = extra_ref[s, 4 * SR + 16 * k : 4 * SR + 16 * (k + 1), :].astype(F32)
                for q in range(2):
                    b = a + 16 * q
                    pr[k, b : b + 16, :] = probe_ref[k, b : b + 16, :] + d[:, q * PS : (q + 1) * PS]

    def place(j):
        r = pos_ref[0, j] - tile_start
        c = pos_ref[1, j]
        base = jnp.where(c >= LN, 1, 0)
        return r, base, c - base * LN

    lanes = lax.broadcasted_iota(jnp.int32, (PS, LN), 1)

    def to_half(j, slot, live):
        r, base, off = place(j)
        head = lanes < LN - off
        turn = (LN - off) & (LN - 1)
        xs = []
        for k in range(2):
            v = [pltpu.roll(x[k, base + q, pl.ds(r, PS), :], turn, 1) for q in range(3)]
            v = jnp.concatenate([jnp.where(head, v[0], v[1]), jnp.where(head, v[1], v[2])], 1)
            patch[slot, k] = v
            xs.append(v)
        xr, xi = xs
        p0, p1 = pr[0], pr[1]
        pg[2] += (xr * xr + xi * xi) * live
        return jnp.concatenate([(p0 * xr - p1 * xi).astype(BF), (p0 * xi + p1 * xr).astype(BF)], 1)

    def half_dot(w, slot):
        for b in range(2):
            half = jnp.dot(w, m1[:, b * PS : (b + 1) * PS], preferred_element_type=F32)
            h[slot, b * PS : (b + 1) * PS, :] = half.astype(BF)

    def far_dot(slot):
        fr = jnp.dot(m2[:PS, :], h[slot], preferred_element_type=F32)
        fi = jnp.dot(m2[PS:, :], h[slot], preferred_element_type=F32)
        return fr, fi

    def update(j, live, far):
        fr, fi = far
        m = jnp.maximum(fr * fr + fi * fi, FLOOR2)
        q = amp_ref[j].astype(F32) * lax.rsqrt(m) - 1.0
        q = q * live
        return jnp.concatenate([(q * fr).astype(BF), (q * fi).astype(BF)], 1)

    def back_half_dot(u, slot):
        for b in range(2):
            half = jnp.dot(u, m2[:, b * PS : (b + 1) * PS], preferred_element_type=F32)
            h2[slot, b * PS : (b + 1) * PS, :] = half.astype(BF)

    def back_dot(slot):
        br = jnp.dot(m1[:PS, :], h2[slot], preferred_element_type=F32)
        bi = jnp.dot(m1[PS:, :], h2[slot], preferred_element_type=F32)
        return br, bi

    def add_back(j, slot, back):
        br, bi = back
        xr, xi = patch[slot, 0], patch[slot, 1]
        pg[0] += xr * br + xi * bi
        pg[1] += xr * bi - xi * br
        p0, p1 = pr[0], pr[1]
        r, base, off = place(j)
        tail = lanes >= off
        turn = off & (LN - 1)
        for k, o in enumerate((p0 * br + p1 * bi, p0 * bi - p1 * br)):
            v = [pltpu.roll(o[:, q * LN : (q + 1) * LN], turn, 1) for q in range(2)]
            g[k, base, pl.ds(r, PS), :] += jnp.where(tail, v[0], 0.0)
            g[k, base + 1, pl.ds(r, PS), :] += jnp.where(tail, v[1], v[0])
            g[k, base + 2, pl.ds(r, PS), :] += jnp.where(tail, 0.0, v[1])

    def visit(i, carry):
        j = [PAIR * i + n for n in range(PAIR)]
        live = [jnp.where(n < count, 1.0, 0.0) for n in j]
        w = to_half(j[0], 0, live[0])
        for n in range(PAIR):
            half_dot(w, n)
            if n + 1 < PAIR:
                w = to_half(j[n + 1], n + 1, live[n + 1])
        fars = [far_dot(n) for n in range(PAIR)]
        us = [update(j[n], live[n], fars[n]) for n in range(PAIR)]
        for n in range(PAIR):
            back_half_dot(us[n], n)
        backs = [back_dot(n) for n in range(PAIR)]
        for n in range(PAIR):
            add_back(j[n], n, backs[n])
        return carry

    lax.fori_loop(0, jnp.minimum((count + PAIR - 1) // PAIR, CAP // PAIR), visit, 0)
    for s in range(NS):
        a = s * SR
        for k in range(2):
            for q in range(4):
                send[s, OWN + k * SR : OWN + (k + 1) * SR, lane_blocks[q]] = g[k, q, a : a + SR, :].astype(BF)
                send[s, NEXT + k * SR : NEXT + (k + 1) * SR, lane_blocks[q]] = g[k, q, TH + a : TH + a + SR, :].astype(BF)
        for k in range(3):
            send[s, PRB + 16 * k : PRB + 16 * (k + 1), :] = jnp.concatenate(
                [pg[k, a : a + 16, :], pg[k, a + 16 : a + 32, :]], 1
            ).astype(BF)
        if first:
            send[s, POS:, :] = extra_ref[...]


def smem():
    return pl.BlockSpec(memory_space=pltpu.SMEM)


def vmem():
    return pl.BlockSpec(memory_space=pltpu.VMEM)


def params(mib):
    return pltpu.CompilerParams(vmem_limit_bytes=mib * 1024 * 1024)


def patterns(pos, cnt, obj, halo, probe, amps, tabs, posblk=None, recv=None):
    first = recv is None
    out = [jax.ShapeDtypeStruct((NS, SEND if first else POS, OW), BF)]
    if not first:
        out += [jax.ShapeDtypeStruct((2, TH, OW), F32), jax.ShapeDtypeStruct((2, PS, PS), F32)]
    args = [pos, cnt, obj, halo, probe, amps, posblk if first else recv, *tabs]
    return pl.pallas_call(
        functools.partial(pattern_kernel, first),
        out_shape=out,
        in_specs=[smem(), smem()] + [vmem()] * 7,
        out_specs=[vmem()] * len(out),
        scratch_shapes=[
            pltpu.VMEM((2, 4, 2 * TH, LN), F32),
            pltpu.VMEM((2, 4, 2 * TH, LN), F32),
            pltpu.VMEM((3, PS, PS), F32),
            pltpu.VMEM((PAIR, 2, PS, PS), F32),
            pltpu.VMEM((PAIR, 2 * PS, PS), BF),
            pltpu.VMEM((PAIR, 2 * PS, PS), BF),
        ],
        compiler_params=params(GRANT),
        name="patterns",
    )(*args)


def sum_kernel(last, recv_ref, own_ref, probe_ref, up_ref, *rest):
    def total(a, n):
        t = [recv_ref[s, a : a + n, :].astype(F32) for s in range(NS)]
        return ((t[0] + t[1]) + (t[2] + t[3])) + ((t[4] + t[5]) + (t[6] + t[7]))

    probe_ref[...] = total(PRB, 48).astype(BF)
    own_ref[...] = total(OWN, 2 * SR)
    up_ref[: 2 * SR, :] = total(NEXT, 2 * SR).astype(BF)
    if not last:
        pos = total(POS, 16)
        rest[0][...] = pos[:, :LN]
        up_ref[2 * SR :, :] = pos.astype(BF)


def sums(last, recv):
    out = [jax.ShapeDtypeStruct((2 * SR, OW), F32), jax.ShapeDtypeStruct((48, OW), BF)]
    if last:
        out += [jax.ShapeDtypeStruct((2 * SR, OW), BF)]
    else:
        out += [jax.ShapeDtypeStruct((2 * SR + 16, OW), BF), jax.ShapeDtypeStruct((16, LN), F32)]
    return pl.pallas_call(
        functools.partial(sum_kernel, last),
        out_shape=out,
        in_specs=[vmem()],
        out_specs=[vmem()] * len(out),
        compiler_params=params(8),
        name="sums",
    )(recv)


def own_kernel(pos_ref, probe_ref, own_ref, up_ref, out_ref, p2, list_ref):
    for q in range(2):
        cols = slice(q * LN, (q + 1) * LN)
        p2[q, :SR, :] = jnp.zeros((SR, LN), F32)
        p2[q, SR + PS :, :] = jnp.zeros((SR, LN), F32)
        p2[q, SR : SR + PS, :] = probe_ref[0, :, cols] * probe_ref[0, :, cols] + probe_ref[1, :, cols] * probe_ref[1, :, cols]
    mine = lax.axis_index("scan") * SR + SR + 1
    lanes = lax.broadcasted_iota(jnp.int32, (8, LN), 1)
    parts = SR // 8

    def group(row, at):
        shift = mine + jnp.where(row < NS, TH, 0)

        def some(i, at):
            for n in range(SOME):
                code = pos_ref[row, SOME * i + n]
                start = shift - code
                list_ref[0, at] = start
                list_ref[1, at] = pos_ref[row, GROUP + SOME * i + n]
                at = at + jnp.where((start > 0) & (start < PS + SR) & (code > 0), 1, 0)
            return at

        return lax.fori_loop(0, (pos_ref[row, 2 * GROUP] + SOME - 1) // SOME, some, at)

    listed = lax.fori_loop(0, 2 * NS, group, 0)
    for n in range(UN):
        list_ref[0, listed + n] = 0
        list_ref[1, listed + n] = 0

    def some(i, carry):
        carry = [list(c) for c in carry]
        for n in range(UN):
            at = list_ref[0, UN * i + n]
            c = list_ref[1, UN * i + n]
            far = c >= LN
            off = jnp.where(far, c - LN, c)
            tail = lanes >= off
            turn = off & (LN - 1)
            for b in range(parts):
                y0, y1 = (pltpu.roll(p2[q, pl.ds(at + 8 * b, 8), :], turn, 1) for q in range(2))
                v = (0.0, jnp.where(tail, y0, 0.0), jnp.where(tail, y1, y0), jnp.where(tail, 0.0, y1), 0.0)
                for q in range(4):
                    carry[b][q] = carry[b][q] + jnp.where(far, v[q], v[q + 1])
        return tuple(tuple(c) for c in carry)

    zero = jnp.zeros((8, LN), F32)
    carry = lax.fori_loop(0, (listed + UN - 1) // UN, some, ((zero,) * 4,) * parts)
    for q in range(4):
        cols = slice(q * LN, (q + 1) * LN)
        scale = 1.0 / (jnp.concatenate([carry[b][q] for b in range(parts)], 0) + REG)
        for k in range(2):
            a = k * SR
            out_ref[a : a + SR, cols] = ((own_ref[a : a + SR, cols] + up_ref[a : a + SR, cols].astype(F32)) * scale).astype(BF)


def own_step(pos, probe, own, up):
    return pl.pallas_call(
        own_kernel,
        out_shape=jax.ShapeDtypeStruct((2 * SR, OW), BF),
        in_specs=[smem(), vmem(), vmem(), vmem()],
        out_specs=vmem(),
        scratch_shapes=[pltpu.VMEM((2, PS + 2 * SR, LN), F32), pltpu.SMEM((2, 2 * NS * CAP + UN), jnp.int32)],
        compiler_params=params(8),
        name="own_step",
    )(pos, probe, own, up)


def spread_kernel(last, *refs):
    *deltas, p0_ref, p1_ref, p2_ref, p3_ref, out_ref = refs
    p = [ref[...].astype(F32) for ref in (p0_ref, p1_ref, p2_ref, p3_ref)]
    probe = (p[0] + p[1]) + (p[2] + p[3])
    w = probe[32:] + REG
    parts = [delta[...] for delta in deltas]
    if last:
        root = jnp.sqrt(w)
        parts += [probe[:16] / root, probe[16:32] / root, root]
    else:
        parts += [probe[:16] / w, probe[16:32] / w]
    at = 0
    for part in parts:
        n = part.shape[0]
        for s in range(NS):
            out_ref[s, at : at + n, :] = part.astype(BF)
        at += n


def spread(last, *args):
    rows = 2 * SR + 48 if last else 4 * SR + 32
    return pl.pallas_call(
        functools.partial(spread_kernel, last),
        out_shape=jax.ShapeDtypeStruct((NS, rows, OW), BF),
        in_specs=[vmem()] * len(args),
        out_specs=vmem(),
        compiler_params=params(8),
        name="spread",
    )(*args)


def final_kernel(obj_ref, probe_ref, recv_ref, obj_out, probe_out, grad_out):
    for s in range(NS):
        a = s * SR
        root = recv_ref[s, 2 * SR + 32 : 2 * SR + 48, :].astype(F32)
        for k in range(2):
            obj_out[k, a : a + SR, :] = obj_ref[k, a : a + SR, :] + recv_ref[s, k * SR : (k + 1) * SR, :].astype(F32)
            grad = recv_ref[s, 2 * SR + 16 * k : 2 * SR + 16 * (k + 1), :].astype(F32)
            d = grad / root
            for q in range(2):
                b = a + 16 * q
                grad_out[k, b : b + 16, :] = grad[:, q * PS : (q + 1) * PS]
                probe_out[k, b : b + 16, :] = probe_ref[k, b : b + 16, :] + d[:, q * PS : (q + 1) * PS]


def final(obj, probe, recv):
    return pl.pallas_call(
        final_kernel,
        out_shape=[
            jax.ShapeDtypeStruct((2, TH, OW), F32),
            jax.ShapeDtypeStruct((2, PS, PS), F32),
            jax.ShapeDtypeStruct((2, PS, PS), F32),
        ],
        in_specs=[vmem()] * 3,
        out_specs=[vmem()] * 3,
        compiler_params=params(8),
        name="final",
    )(obj, probe, recv)


def shifted(block, distance):
    return lax.ppermute(block, "tile", [(i, (i + distance) % NT) for i in range(NT)])


def swapped(block, bits):
    return lax.ppermute(block, "tile", [(i, i ^ bits) for i in range(NT)])


def two(x, swap):
    return (x.astype(F32) + swap.astype(F32)).astype(BF)


def four(x, swaps):
    y = [swap.astype(F32) for swap in swaps]
    return ((x.astype(F32) + y[0]) + (y[1] + y[2])).astype(BF)


def exchange(blocks):
    return lax.all_to_all(blocks, "scan", 0, 0, tiled=True)


def on_device(object_field, probe, amplitudes, positions, counts):
    pos = positions[0, 0].T
    cnt = counts[0, 0].reshape(1)
    amps, *tabs = prepare(amplitudes[0, 0])
    halo = shifted(object_field.astype(BF), -1)
    live = lax.broadcasted_iota(jnp.int32, (CAP,), 0) < cnt
    row = jnp.concatenate([jnp.where(live, pos[0] - lax.axis_index("tile") * TH + 1, 0), pos[1], cnt])
    mine = lax.broadcasted_iota(jnp.int32, (16, 1), 0) == lax.axis_index("scan")
    posblk = jnp.where(mine, row[None, :], 0).astype(BF)
    posblk = jnp.pad(posblk, ((0, 0), (0, OW - row.shape[0])))
    coded = 2 * GROUP + 1
    (send,) = patterns(pos, cnt, object_field, halo, probe, amps, tabs, posblk=posblk)
    own, part, up, tile_pos = sums(False, exchange(send))
    core = swapped(part, 1)
    up = shifted(up, 1)
    part = two(part, core)
    swaps = [swapped(part, d) for d in (2, 16, 18)]
    around = jnp.concatenate([up[2 * SR :, :coded][:NS].astype(F32), tile_pos[:NS, :coded]], 0).astype(jnp.int32)
    delta = own_step(around, probe, own, up)
    part = four(part, swaps)
    swaps = [swapped(part, d) for d in (4, 8, 12)]
    recv = exchange(spread(False, delta, shifted(delta, -1), part, *swaps))
    send, object_field, probe = patterns(pos, cnt, object_field, halo, probe, amps, tabs, recv=recv)
    own, part, up = sums(True, exchange(send))
    core = swapped(part, 1)
    up = shifted(up, 1)
    part = two(part, core)
    swaps = [swapped(part, d) for d in (2, 16, 18)]
    delta = own_step(around, probe, own, up)
    part = four(part, swaps)
    swaps = [swapped(part, d) for d in (4, 8, 12)]
    recv = exchange(spread(True, delta, part, *swaps))
    return tuple(final(object_field, probe, recv))


def solution(mesh):
    in_specs = (
        P(None, "tile", None),
        P(),
        P("scan", "tile", None, None, None),
        P("scan", "tile", None, None),
        P("scan", "tile"),
    )
    out_specs = (P(None, "tile", None), P(), P())
    return jax.shard_map(on_device, mesh=mesh, in_specs=in_specs, out_specs=out_specs, check_vma=False)
```
